128 devices in a mesh: row: 4 (over y_hi, core), col: 4 (over z), dp: 8 (over y_lo, x).
Axes of the slice: x: 4, y: 4 (y_hi: 2, y_lo: 2; y = y_hi * 2 + y_lo), z: 4, core: 2. Of those that a mesh axis runs over, the one named last changes fastest.
Arguments:
- observed: bfloat16 [4096, 2048], P(('row', 'dp'), 'col'), may hold values from -6 to 6
- next_observed: bfloat16 [4096, 2048], P(('row', 'dp'), 'col'), may hold values from -6 to 6
- actions: bfloat16 [4096, 128], P(('row', 'dp')), may hold values from -1 to 1
- next_mean: bfloat16 [4096, 128], P(('row', 'dp')), may hold values from -1.1953125 to 1.1953125
- policy_noise: float32 [4096, 128], P(('row', 'dp')), may hold values from -1.5 to 1.5
- rewards: bfloat16 [4096], P(('row', 'dp')), may hold values from -5 to 5
- discounts: bfloat16 [4096], P(('row', 'dp')), may hold values from 0.5 to 0.98828125
- actor_flags: int32 [4096], P(('row', 'dp')), may hold values 0 or 1
- critic_in: float32 [2, 2048, 2048], P(None, 'col', 'row'), may hold values from -0.125 to 0.125
- critic_act: float32 [2, 128, 2048], P(None, None, 'col'), may hold values from -0.5 to 0.5
- critic_head: float32 [2, 2048], P(None, 'row'), may hold values from -0.125 to 0.125
- target_in: float32 [2, 2048, 2048], P(None, 'col', 'row'), may hold values from -0.125 to 0.125
- target_act: float32 [2, 128, 2048], P(None, None, 'col'), may hold values from -0.5 to 0.5
- target_head: float32 [2, 2048], P(None, 'row'), may hold values from -0.125 to 0.125
Outputs:
- new_in: float32 [2, 2048, 2048], P(None, 'col', 'row')
- new_act: float32 [2, 128, 2048], P(None, None, 'col')
- new_head: float32 [2, 2048], P(None, 'row')
- new_target_in: float32 [2, 2048, 2048], P(None, 'col', 'row')
- new_target_act: float32 [2, 128, 2048], P(None, None, 'col')
- new_target_head: float32 [2, 2048], P(None, 'row')
- temporal_errors: float32 [2, 4096], P(None, ('row', 'dp'))
- action_slope: float32 [4096, 128], P(('row', 'dp'))
The draws below stay inside these ranges and needn't reach their ends.
All inputs are finite; a program needn't handle non-finite values. No bound on the sum of `actor_flags` on one device may be relied on, other than what follows from the above.
Results may differ from the reference program's by a relative error of at most 0.008.
Values may be sent and summed in bfloat16 or wider, within the bound.
No kernel may reach another device: no remote copies, remote signals or barrier semaphores. Data moves between devices by JAX's collectives and lax.ppermute only.
A program may use at most 128 MiB of HBM per device.

```python
import jax
import jax.numpy as jnp
from jax import lax

D = 2048
ACT = 128
TOKENS = 4096


def place_ends(drawn, rng, smallest, high):
    shape = drawn.shape
    index_at = [jax.random.randint(jax.random.fold_in(rng, axis), (), 0, shape[axis]) for axis in range(len(shape))]
    drawn = drawn.at[tuple(index_at)].set(smallest)
    longest = shape.index(max(shape))
    index_at[longest] = (index_at[longest] + 1) % shape[longest]
    return drawn.at[tuple(index_at)].set(high)


def level_of(key, dims, split, low, high):
    def one(dim, parts):
        draws = jax.random.uniform(jax.random.fold_in(jax.random.fold_in(key, 6), dim), (parts,), jnp.float32, low / len(split), high / len(split))
        return jnp.repeat(jnp.exp(draws), dims[dim] // parts).reshape((-1,) + (1,) * (len(dims) - dim - 1))

    factor_of = one(*split[0])
    for cut in split[1:]:
        factor_of = factor_of * one(*cut)
    return factor_of


def gaussian(own_key, shape, width, reach, pieces=(), held_as=jnp.bfloat16):
    values = jax.random.normal(own_key, shape, jnp.float32) * width
    if len(pieces) > 0:
        values = level_of(own_key, shape, pieces, -0.22, 0.18) * values
    return jnp.clip(values, min=-reach, max=reach).astype(held_as)


def setup_inputs(seed: int = 0) -> dict:
    seeds = jax.random.split(jax.random.key(seed), 15)
    return {
        "observed": gaussian(seeds[0], (TOKENS, D), 1.0, 6.0, ((0, 32), (1, 4))),
        "next_observed": gaussian(seeds[1], (TOKENS, D), 1.0, 6.0, ((0, 32), (1, 4))),
        "actions": jnp.clip(jax.random.uniform(seeds[2], (TOKENS, ACT), jnp.float32, -1.0, 1.0) * level_of(seeds[2], (TOKENS, ACT), ((0, 32),), -0.4, 0.0), -1.0, 1.0).astype(jnp.bfloat16),
        "next_mean": jnp.clip(jax.random.uniform(seeds[3], (TOKENS, ACT), jnp.float32, -1.1953125, 1.1953125) * level_of(seeds[3], (TOKENS, ACT), ((0, 32),), -0.4, 0.0), -1.1953125, 1.1953125).astype(jnp.bfloat16),
        "policy_noise": gaussian(seeds[4], (TOKENS, ACT), 0.3, 1.5, ((0, 32),), jnp.float32),
        "rewards": gaussian(seeds[5], (TOKENS,), 1.0, 5.0, ((0, 32),)),
        "discounts": jnp.clip(0.5 + 0.48828125 * jax.random.uniform(seeds[6], (TOKENS,), jnp.float32) ** level_of(seeds[6], (TOKENS,), ((0, 32),), -0.2, 0.2), 0.5, 0.98828125).astype(jnp.bfloat16),
        "actor_flags": place_ends((jax.random.randint(seeds[7], (TOKENS,), 0, 2) < 1).astype(jnp.int32), jax.random.fold_in(seeds[7], 1), 0, 1),
        "critic_in": gaussian(seeds[8], (2, D, D), D ** -0.5, 0.125, ((1, 4), (2, 4)), jnp.float32),
        "critic_act": gaussian(seeds[9], (2, ACT, D), ACT ** -0.5, 0.5, ((2, 4),), jnp.float32),
        "critic_head": gaussian(seeds[10], (2, D), D ** -0.5, 0.125, ((1, 4),), jnp.float32),
        "target_in": gaussian(seeds[11], (2, D, D), D ** -0.5, 0.125, ((1, 4), (2, 4)), jnp.float32),
        "target_act": gaussian(seeds[12], (2, ACT, D), ACT ** -0.5, 0.5, ((2, 4),), jnp.float32),
        "target_head": gaussian(seeds[13], (2, D), D ** -0.5, 0.125, ((1, 4),), jnp.float32),
    }


noise_clip = 0.5
matrix_rate = 0.004
head_rate = 0.0001
blend_rate = 0.005


def silu_slope(preact):
    sigma = jax.nn.sigmoid(preact)
    return sigma * (1.0 + preact * (1.0 - sigma))


def forward(states, moves, weight_in, weight_act, weight_head):
    embedded = (states.astype(jnp.float32) + jnp.dot(moves, weight_act.astype(jnp.bfloat16), preferred_element_type=jnp.float32)).astype(jnp.bfloat16)
    preact = jnp.dot(embedded, weight_in.astype(jnp.bfloat16), preferred_element_type=jnp.float32)
    hidden = jax.nn.silu(preact)
    value = jnp.dot(hidden, weight_head, precision=lax.Precision.HIGHEST)
    return embedded, preact, hidden, value


def reference(observed, next_observed, actions, next_mean, policy_noise, rewards, discounts, actor_flags, critic_in, critic_act, critic_head, target_in, target_act, target_head):
    noisy = jnp.clip(next_mean.astype(jnp.float32) + jnp.clip(policy_noise, -noise_clip, noise_clip), -1.0, 1.0).astype(jnp.bfloat16)
    target_zero = forward(next_observed, noisy, target_in[0], target_act[0], target_head[0])[3]
    target_one = forward(next_observed, noisy, target_in[1], target_act[1], target_head[1])[3]
    goal = rewards.astype(jnp.float32) + discounts.astype(jnp.float32) * jnp.minimum(target_zero, target_one)
    fresh_in = []
    fresh_act = []
    fresh_head = []
    errors = []
    action_slope = None
    for which in range(2):
        embedded, preact, hidden, value = forward(observed, actions, critic_in[which], critic_act[which], critic_head[which])
        error = value - goal
        slope = (critic_head[which] * silu_slope(preact)).astype(jnp.bfloat16)
        delta = (2.0 * error[:, None] * slope.astype(jnp.float32)).astype(jnp.bfloat16)
        back = jnp.dot(slope, critic_in[which].astype(jnp.bfloat16).T, preferred_element_type=jnp.float32)
        grad_embedded = (2.0 * error[:, None] * back).astype(jnp.bfloat16)
        grad_in = jnp.dot(embedded.T, delta, preferred_element_type=jnp.float32)
        grad_act = jnp.dot(actions.T, grad_embedded, preferred_element_type=jnp.float32)
        grad_head = jnp.dot(2.0 * error, hidden, precision=lax.Precision.HIGHEST)
        fresh_in.append(critic_in[which] - matrix_rate * grad_in)
        fresh_act.append(critic_act[which] - matrix_rate * grad_act)
        fresh_head.append(critic_head[which] - head_rate * grad_head)
        errors.append(error)
        if which == 0:
            push = jnp.dot(back.astype(jnp.bfloat16), critic_act[0].astype(jnp.bfloat16).T, preferred_element_type=jnp.float32)
            action_slope = actor_flags.astype(jnp.float32)[:, None] * push
    new_in = jnp.stack(fresh_in)
    new_act = jnp.stack(fresh_act)
    new_head = jnp.stack(fresh_head)
    new_target_in = blend_rate * new_in + (1.0 - blend_rate) * target_in
    new_target_act = blend_rate * new_act + (1.0 - blend_rate) * target_act
    new_target_head = blend_rate * new_head + (1.0 - blend_rate) * target_head
    return new_in, new_act, new_head, new_target_in, new_target_act, new_target_head, jnp.stack(errors), action_slope
```

```python
import jax
import jax.numpy as jnp
from jax import lax
from jax.experimental import pallas as pl
from jax.experimental.pallas import tpu as pltpu
from jax.sharding import PartitionSpec as P

noise_clip = 0.5
matrix_rate = 0.004
head_rate = 0.0001
blend_rate = 0.005

bf16 = jnp.bfloat16
f32 = jnp.float32

VMEM = pl.BlockSpec(memory_space=pltpu.VMEM)
SMEM = pl.BlockSpec(memory_space=pltpu.SMEM)


def call(body, outs, ins, scratch=(), scalars=None, mib=16, flops=0, name=None):
    specs = [VMEM] * len(ins)
    if scalars is not None:
        ins = [scalars, *ins]
        specs = [SMEM, *specs]
    moved = sum(a.size * a.dtype.itemsize for a in ins)
    moved += sum(o.size * o.dtype.itemsize for o in outs)
    return pl.pallas_call(
        body,
        out_shape=tuple(outs),
        in_specs=specs,
        out_specs=tuple(VMEM for _ in outs),
        scratch_shapes=list(scratch),
        compiler_params=pltpu.CompilerParams(vmem_limit_bytes=mib * 2**20),
        cost_estimate=pl.CostEstimate(flops=flops, bytes_accessed=moved, transcendentals=0),
        name=name,
    )(*ins)


def shape(*dims, dtype=bf16):
    return jax.ShapeDtypeStruct(dims, dtype)


def dot(a, b):
    return jnp.dot(a, b, preferred_element_type=f32)


def swap(x, axis, bit):
    n = lax.axis_size(axis)
    return lax.ppermute(x, axis, [(i, i ^ bit) for i in range(n)])


def pack_body(obs, nxt, act, mean, noise, out):
    out[:, 0:512] = obs[...]
    out[:, 512:1024] = nxt[...]
    out[:, 1024:1152] = act[...]
    clipped = jnp.clip(noise[...], -noise_clip, noise_clip)
    out[:, 1152:1280] = jnp.clip(mean[...].astype(f32) + clipped, -1.0, 1.0).astype(bf16)


def weights_body(cin, tin, cact, tact, w, a, p):
    for k in range(2):
        w[k] = cin[k].astype(bf16)
        w[2 + k] = tin[k].astype(bf16)
        a[k] = cact[k].astype(bf16)
        a[2 + k] = tact[k].astype(bf16)
    p[...] = dot(a[0], w[0]).T.astype(bf16)


def forward_body(at, x0, x1, a, w, mine, out1, out2, out3, emb, acts, xs, part):
    core, col = at[0], at[1]
    xs[pl.ds(pl.multiple_of(core * 128, 128), 128), :] = x0[...]
    xs[pl.ds(pl.multiple_of((1 - core) * 128, 128), 128), :] = x1[...]
    for q in range(4):
        s = 0 if q < 2 else 512
        m = 1024 if q < 2 else 1152
        e = (xs[:, s : s + 512].astype(f32) + dot(xs[:, m : m + 128], a[q])).astype(bf16)
        if q < 2:
            emb[q] = e
        part[:, 512 * q : 512 * q + 512] = dot(e, w[q])
    acts[...] = xs[:, 1024:1152]

    def rows(k):
        return pl.ds(pl.multiple_of((col ^ k) * 64, 64), 64)

    mine[...] = part[rows(0), :]
    out1[...] = part[rows(1), :].astype(bf16)
    out2[...] = part[rows(2), :].astype(bf16)
    out3[...] = part[rows(3), :].astype(bf16)


def turn_body(emb1, emb2, acts1, acts2, left):
    for k in range(2):
        left[k, 0:512, 0:256] = emb1[k].T
        left[k, 0:512, 256:512] = emb2[k].T
        left[k, 512:640, 0:256] = acts1[...].T
        left[k, 512:640, 256:512] = acts2[...].T


def hidden_body(at, m1, r11, r12, r13, m2, r21, r22, r23, heads, rew, slope, hidden, packet, vals):
    y_hi = at[2]
    vals[...] = jnp.zeros_like(vals)
    for half, (m, r1, r2, r3) in enumerate(((m1, r11, r12, r13), (m2, r21, r22, r23))):
        rows = slice(64 * half, 64 * half + 64)
        for q in range(4):
            cols = slice(512 * q, 512 * q + 512)
            pre = (m[:, cols] + r1[:, cols].astype(f32)) + (
                r2[:, cols].astype(f32) + r3[:, cols].astype(f32)
            )
            sig = jax.nn.sigmoid(pre)
            hid = pre * sig
            v = heads[q : q + 1, :]
            vals[rows, q : q + 1] = jnp.sum(hid * v, axis=1, keepdims=True)
            if q < 2:
                hidden[rows, cols] = hid
                slope[rows, cols] = (v * (sig * (1.0 + pre * (1.0 - sig)))).astype(bf16)
    turned = vals[...].T[0:8, :]
    swapped = jnp.concatenate([turned[:, 64:128], turned[:, 0:64]], axis=1)
    turned = jnp.where(y_hi == 1, swapped, turned)
    line = lax.broadcasted_iota(jnp.int32, (8, 128), 0)
    turned = jnp.where(line < 4, turned, rew[...])
    for i in range(16):
        packet[i] = turned


def grads_body(
    at, s0, s1, s2, s3, got, left, hidden, p,
    o0, o1, o2, o3, o4, o5, o6, o7, keep, give, terr,
    delta, slope0, grad, errs,
):
    core, col, y_hi, dp = at[0], at[1], at[2], at[3]
    for c in range(4):
        v = (got[c] + got[4 + c]) + (got[8 + c] + got[12 + c])
        lanes = slice(64 * (c % 2), 64 * (c % 2) + 64)
        both = jnp.concatenate([got[c // 2 * 4][:, lanes], got[(2 + c // 2) * 4][:, lanes]], axis=1)
        goal = both[4:5] + both[5:6] * jnp.minimum(v[2:3], v[3:4])
        e = v[0:2] - goal
        e = jnp.where(y_hi == 1, jnp.concatenate([e[:, 64:128], e[:, 0:64]], axis=1), e)
        errs[c, 0:2, :] = e
    lo = jnp.concatenate([errs[0, 0:2, 0:64], errs[1, 0:2, 0:64]], axis=1)
    hi = jnp.concatenate([errs[2, 0:2, 0:64], errs[3, 0:2, 0:64]], axis=1)
    terr[...] = jnp.where(core == 1, hi, lo)
    for k, s in enumerate((s0, s1, s2, s3)):
        c = col ^ k
        block = jnp.concatenate([errs[c], jnp.zeros((120, 128), f32)], axis=0)
        e = 2.0 * block.T
        for half in range(2):
            rows = slice(64 * half, 64 * half + 64)
            to = pl.ds(pl.multiple_of(256 * half + 64 * c, 64), 64)
            slope0[to, :] = s[rows, 0:512]
            for q in range(2):
                cols = slice(512 * q, 512 * q + 512)
                delta[q, to, :] = (e[rows, q : q + 1] * s[rows, cols].astype(f32)).astype(bf16)
        if k == 0:
            heads = [
                jnp.sum(e[:, q : q + 1] * hidden[:, 512 * q : 512 * q + 512], axis=0, keepdims=True)
                for q in range(2)
            ]
    for q in range(2):
        grad[q] = dot(left[q], delta[q])
    tail = jnp.concatenate([*heads, jnp.zeros((14, 512), f32)], axis=0).astype(bf16)
    for k, o in enumerate((o0, o1, o2, o3, o4, o5, o6, o7)):
        d = dp ^ k
        wide = pl.ds(pl.multiple_of(64 * d, 64), 64)
        thin = pl.ds(pl.multiple_of(512 + 16 * d, 16), 16)
        o[0:64, :] = grad[0, wide, :].astype(bf16)
        o[64:128, :] = grad[1, wide, :].astype(bf16)
        o[128:144, :] = grad[0, thin, :].astype(bf16)
        o[144:160, :] = grad[1, thin, :].astype(bf16)
        o[160:176, :] = tail
    push = dot(slope0[...], p[...])
    first, second = push[0:128], push[128:256]
    keep[0] = jnp.where(core == 1, second, first)
    give[0] = jnp.where(core == 1, first, second)
    first, second = push[256:384], push[384:512]
    keep[1] = jnp.where(core == 1, second, first)
    give[1] = jnp.where(core == 1, first, second)


def total_body(c0, c1, c2, c3, c4, c5, c6, c7, w, chunk, act, head):
    def at(rows):
        x = [c[rows, :].astype(f32) for c in (c0, c1, c2, c3, c4, c5, c6, c7)]
        return ((x[0] + x[1]) + (x[2] + x[3])) + ((x[4] + x[5]) + (x[6] + x[7]))

    chunk[...] = at(slice(0, 128)).astype(bf16)
    head[...] = at(slice(160, 168))
    for q in range(2):
        m = at(slice(128 + 16 * q, 144 + 16 * q)).astype(bf16)
        act[16 * q : 16 * q + 16, :] = lax.dot_general(
            m, w[q], (((1,), (1,)), ((), ())), preferred_element_type=f32
        )


def update_body(at, g0, g1, g2, g3, g4, g5, g6, g7, cin, tin, fresh, blended):
    dp = at[3]
    for k, g in enumerate((g0, g1, g2, g3, g4, g5, g6, g7)):
        rows = pl.ds(pl.multiple_of(64 * (dp ^ k), 64), 64)
        for q in range(2):
            new = cin[q, rows, :] - matrix_rate * g[64 * q : 64 * q + 64, :].astype(f32)
            fresh[q, rows, :] = new
            blended[q, rows, :] = blend_rate * new + (1.0 - blend_rate) * tin[q, rows, :]


def on_device(
    observed,
    next_observed,
    actions,
    next_mean,
    policy_noise,
    rewards,
    discounts,
    actor_flags,
    critic_in,
    critic_act,
    critic_head,
    target_in,
    target_act,
    target_head,
):
    row, col, dp = lax.axis_index("row"), lax.axis_index("col"), lax.axis_index("dp")
    at = jnp.stack([row % 2, col, row // 2, dp]).astype(jnp.int32)

    (own,) = call(
        pack_body, [shape(128, 1280)],
        [observed, next_observed, actions, next_mean, policy_noise], name="pack",
    )
    sib = swap(own, "row", 1)
    far = swap(own, "row", 2)
    w16, a16, p16 = call(
        weights_body,
        [shape(4, 512, 512), shape(4, 128, 512), shape(512, 128)],
        [critic_in, target_in, critic_act, target_act],
        mib=24, flops=2 * 128 * 512 * 512, name="weights",
    )

    def forward(x0, x1, name):
        return call(
            forward_body,
            [
                shape(64, 2048, dtype=f32), shape(64, 2048), shape(64, 2048), shape(64, 2048),
                shape(2, 256, 512), shape(256, 128),
            ],
            [x0, x1, a16, w16],
            scratch=[pltpu.VMEM((256, 1280), bf16), pltpu.VMEM((256, 2048), f32)],
            scalars=at, mib=24, flops=8 * 256 * 640 * 512, name=name,
        )

    mine1, *out1, emb1, acts1 = forward(own, sib, "forward_near")
    in1 = [swap(x, "col", k + 1) for k, x in enumerate(out1)]
    farsib = swap(far, "row", 1)
    mine2, *out2, emb2, acts2 = forward(far, farsib, "forward_far")
    in2 = [swap(x, "col", k + 1) for k, x in enumerate(out2)]
    (left,) = call(
        turn_body, [shape(2, 640, 512)], [emb1, emb2, acts1, acts2], name="turn"
    )
    heads = jnp.concatenate(
        [critic_head, target_head, jnp.zeros((4, 512), f32)], axis=0
    )
    blank = jnp.zeros((1, 128), f32)
    rew = jnp.concatenate(
        [blank, blank, blank, blank, rewards.astype(f32)[None], discounts.astype(f32)[None], blank, blank]
    )
    slope, hidden, packet = call(
        hidden_body,
        [shape(128, 1024), shape(128, 1024, dtype=f32), shape(16, 8, 128, dtype=f32)],
        [mine1, *in1, mine2, *in2, heads, rew],
        scratch=[pltpu.VMEM((128, 128), f32)],
        scalars=at, name="hidden", flops=128 * 2048 * 30,
    )
    slopes = [slope] + [swap(slope, "col", k) for k in (1, 2, 3)]
    got = lax.all_to_all(packet, ("row", "col"), 0, 0, tiled=True)
    *chunks, keep, give, temporal_errors = call(
        grads_body,
        [shape(176, 512)] * 8
        + [shape(2, 128, 128, dtype=f32), shape(2, 128, 128, dtype=f32), shape(2, 128, dtype=f32)],
        [*slopes, got, left, hidden, p16],
        scratch=[
            pltpu.VMEM((2, 512, 512), bf16), pltpu.VMEM((512, 512), bf16),
            pltpu.VMEM((2, 640, 512), f32), pltpu.VMEM((4, 8, 128), f32),
        ],
        scalars=at, mib=24, name="grads", flops=4 * 640 * 512 * 512,
    )
    summed = [chunks[0]] + [swap(chunks[k], "dp", k) for k in range(1, 8)]
    push = keep + swap(give, "row", 1)
    push = push[0] + swap(push[1], "row", 2)
    push = push + swap(push, "col", 1)
    push = push + swap(push, "col", 2)
    action_slope = actor_flags.astype(f32)[:, None] * push

    chunk, act, head = call(
        total_body,
        [shape(128, 512), shape(32, 512, dtype=f32), shape(8, 512, dtype=f32)],
        [*summed, w16], name="total", flops=4 * 16 * 512 * 512,
    )
    parts = [chunk] + [swap(chunk, "dp", k) for k in range(1, 8)]
    act = act + swap(act, "row", 1)
    act = act + swap(act, "row", 2)
    head = head + swap(head, "col", 1)
    head = head + swap(head, "col", 2)
    acts = lax.all_to_all(
        jnp.broadcast_to(act.astype(bf16), (8, 32, 512)), "dp", 0, 0, tiled=True
    )
    grad_act = acts.reshape(8, 2, 16, 512).swapaxes(0, 1).reshape(2, 128, 512).astype(f32)

    new_in, new_target_in = call(
        update_body,
        [shape(2, 512, 512, dtype=f32)] * 2,
        [*parts, critic_in, target_in],
        scalars=at, mib=24, name="update",
    )
    new_act = critic_act - matrix_rate * grad_act
    new_target_act = blend_rate * new_act + (1.0 - blend_rate) * target_act
    new_head = critic_head - head_rate * head[0:2]
    new_target_head = blend_rate * new_head + (1.0 - blend_rate) * target_head
    return (
        new_in,
        new_act,
        new_head,
        new_target_in,
        new_target_act,
        new_target_head,
        temporal_errors,
        action_slope,
    )


def solution(mesh):
    return jax.shard_map(
        on_device,
        mesh=mesh,
        in_specs=(
            P(("row", "dp"), "col"),
            P(("row", "dp"), "col"),
            P(("row", "dp"), None),
            P(("row", "dp"), None),
            P(("row", "dp"), None),
            P(("row", "dp")),
            P(("row", "dp")),
            P(("row", "dp")),
            P(None, "col", "row"),
            P(None, None, "col"),
            P(None, "row"),
            P(None, "col", "row"),
            P(None, None, "col"),
            P(None, "row"),
        ),
        out_specs=(
            P(None, "col", "row"),
            P(None, None, "col"),
            P(None, "row"),
            P(None, "col", "row"),
            P(None, None, "col"),
            P(None, "row"),
            P(None, ("row", "dp")),
            P(("row", "dp"), None),
        ),
        check_vma=False,
    )
```

```python
import jax
import jax.numpy as jnp
from jax import lax
from jax.experimental import pallas as pl
from jax.experimental.pallas import tpu as pltpu
from jax.sharding import PartitionSpec as P

noise_clip = 0.5
matrix_rate = 0.004
head_rate = 0.0001
blend_rate = 0.005

bf16 = jnp.bfloat16
f32 = jnp.float32

SPECS = {m: pl.BlockSpec(memory_space=m) for m in (pltpu.VMEM, pltpu.SMEM, pltpu.HBM)}
ANY = pl.BlockSpec(memory_space=pl.ANY)
DMA = pltpu.SemaphoreType.DMA
VMEM, HBM = pltpu.VMEM, pltpu.HBM


def call(
    body, outs, ins, scratch=(), scalars=None, mib=16, flops=0, name=None,
    where=(), to=(), raw=(), aliases=None,
):
    moved = sum(a.size * a.dtype.itemsize for a in ins)
    moved += sum(o.size * o.dtype.itemsize for o in outs)
    raw_out = to == "raw"
    to = range(len(outs)) if raw_out else to
    specs = [SPECS[HBM if i in raw else VMEM] for i in range(len(ins))]
    ins = [
        pltpu.with_memory_space_constraint(a, HBM) if i in raw or i in where else a
        for i, a in enumerate(ins)
    ]
    if scalars is not None:
        ins = [scalars, *ins]
        specs = [SPECS[pltpu.SMEM], *specs]
    return pl.pallas_call(
        body,
        out_shape=tuple(HBM(o.shape, o.dtype) if i in to else o for i, o in enumerate(outs)),
        in_specs=specs,
        out_specs=tuple(SPECS[HBM if raw_out else VMEM] for _ in outs),
        scratch_shapes=list(scratch),
        input_output_aliases=aliases or {},
        compiler_params=pltpu.CompilerParams(vmem_limit_bytes=mib * 2**20),
        cost_estimate=pl.CostEstimate(flops=flops, bytes_accessed=moved, transcendentals=0),
        name=name,
    )(*ins)


def after(x, other):
    return pl.pallas_call(
        lambda x, other, out: None,
        out_shape=jax.ShapeDtypeStruct(x.shape, x.dtype),
        in_specs=[ANY, ANY],
        out_specs=ANY,
        input_output_aliases={0: 0},
        name="after",
    )(x, other)


def shape(*dims, dtype=bf16):
    return jax.ShapeDtypeStruct(dims, dtype)


def dot(a, b):
    return jnp.dot(a, b, preferred_element_type=f32)


def swap(x, axis, bit):
    n = lax.axis_size(axis)
    return lax.ppermute(x, axis, [(i, i ^ bit) for i in range(n)])


def pack_body(obs, nxt, act, mean, noise, out, means, noises, sems):
    copies = [
        pltpu.make_async_copy(src, dst, sems.at[i])
        for i, (src, dst) in enumerate(
            (
                (mean, means),
                (noise, noises),
                (obs, out.at[:, 0:512]),
                (nxt, out.at[:, 512:1024]),
                (act, out.at[:, 1024:1152]),
            )
        )
    ]
    for c in copies:
        c.start()
    copies[0].wait()
    copies[1].wait()
    clipped = jnp.clip(noises[...], -noise_clip, noise_clip)
    out[:, 1152:1280] = jnp.clip(means[...].astype(f32) + clipped, -1.0, 1.0).astype(bf16)
    for c in copies[2:]:
        c.wait()


def weights_body(cin, tin, cact, tact, w, a, p, wide, thin, sems):
    pairs = []
    for k in range(2):
        pairs.append((cact.at[k], thin.at[k]))
        pairs.append((cin.at[k], wide.at[k]))
    for k in range(2):
        pairs.append((tact.at[k], thin.at[2 + k]))
        pairs.append((tin.at[k], wide.at[2 + k]))
    copies = [pltpu.make_async_copy(src, dst, sems.at[i]) for i, (src, dst) in enumerate(pairs)]
    for c in copies:
        c.start()
    for k in range(4):
        copies[2 * k].wait()
        a[k] = thin[k].astype(bf16)
        copies[2 * k + 1].wait()
        w[k] = wide[k].astype(bf16)
        if k == 0:
            p[...] = dot(a[0], w[0]).T.astype(bf16)


def forward_body(at, x0, x1, a, w, mine, out1, out2, out3, left, xs, part):
    core, col = at[0], at[1]
    xs[pl.ds(pl.multiple_of(core * 128, 128), 128), :] = x0[...]
    xs[pl.ds(pl.multiple_of((1 - core) * 128, 128), 128), :] = x1[...]
    turned = xs[:, 1024:1152].T
    for q in range(4):
        s = 0 if q < 2 else 512
        m = 1024 if q < 2 else 1152
        e = (xs[:, s : s + 512].astype(f32) + dot(xs[:, m : m + 128], a[q])).astype(bf16)
        if q < 2:
            left[q, 0:512, :] = e.T
            left[q, 512:640, :] = turned
        part[:, 512 * q : 512 * q + 512] = dot(e, w[q])

    def rows(k):
        return pl.ds(pl.multiple_of((col ^ k) * 64, 64), 64)

    mine[...] = part[rows(0), :]
    out1[...] = part[rows(1), :].astype(bf16)
    out2[...] = part[rows(2), :].astype(bf16)
    out3[...] = part[rows(3), :].astype(bf16)


def hidden_body(at, m1, r11, r12, r13, m2, r21, r22, r23, heads, rew, slope, hidden, packet, vals):
    y_hi = at[2]
    vals[...] = jnp.zeros_like(vals)
    for half, (m, r1, r2, r3) in enumerate(((m1, r11, r12, r13), (m2, r21, r22, r23))):
        rows = slice(64 * half, 64 * half + 64)
        for q in range(4):
            cols = slice(512 * q, 512 * q + 512)
            pre = (m[:, cols] + r1[:, cols].astype(f32)) + (
                r2[:, cols].astype(f32) + r3[:, cols].astype(f32)
            )
            sig = jax.nn.sigmoid(pre)
            hid = pre * sig
            v = heads[q : q + 1, :]
            vals[rows, q : q + 1] = jnp.sum(hid * v, axis=1, keepdims=True)
            if q < 2:
                hidden[rows, cols] = hid
                slope[rows, cols] = (v * (sig * (1.0 + pre * (1.0 - sig)))).astype(bf16)
    turned = vals[...].T[0:8, :]
    swapped = jnp.concatenate([turned[:, 64:128], turned[:, 0:64]], axis=1)
    turned = jnp.where(y_hi == 1, swapped, turned)
    line = lax.broadcasted_iota(jnp.int32, (8, 128), 0)
    turned = jnp.where(line < 4, turned, rew[...])
    for i in range(16):
        packet[i] = turned


def grads_body(
    at, s0, s1, s2, s3, got, left1, left2, hidden, p,
    out, keep, give, terr,
    delta, slope0, grad, errs,
):
    core, col, y_hi, dp = at[0], at[1], at[2], at[3]
    for c in range(4):
        v = (got[c] + got[4 + c]) + (got[8 + c] + got[12 + c])
        lanes = slice(64 * (c % 2), 64 * (c % 2) + 64)
        both = jnp.concatenate([got[c // 2 * 4][:, lanes], got[(2 + c // 2) * 4][:, lanes]], axis=1)
        goal = both[4:5] + both[5:6] * jnp.minimum(v[2:3], v[3:4])
        e = v[0:2] - goal
        e = jnp.where(y_hi == 1, jnp.concatenate([e[:, 64:128], e[:, 0:64]], axis=1), e)
        errs[c, 0:2, :] = e
    lo = jnp.concatenate([errs[0, 0:2, 0:64], errs[1, 0:2, 0:64]], axis=1)
    hi = jnp.concatenate([errs[2, 0:2, 0:64], errs[3, 0:2, 0:64]], axis=1)
    terr[...] = jnp.where(core == 1, hi, lo)
    for k, s in enumerate((s0, s1, s2, s3)):
        c = col ^ k
        block = jnp.concatenate([errs[c], jnp.zeros((120, 128), f32)], axis=0)
        e = 2.0 * block.T
        for half in range(2):
            rows = slice(64 * half, 64 * half + 64)
            to = pl.ds(pl.multiple_of(256 * half + 64 * c, 64), 64)
            slope0[to, :] = s[rows, 0:512]
            for q in range(2):
                cols = slice(512 * q, 512 * q + 512)
                delta[q, to, :] = (e[rows, q : q + 1] * s[rows, cols].astype(f32)).astype(bf16)
        if k == 0:
            heads = [
                jnp.sum(e[:, q : q + 1] * hidden[:, 512 * q : 512 * q + 512], axis=0, keepdims=True)
                for q in range(2)
            ]
    for q in range(2):
        grad[q] = dot(left1[q], delta[q, 0:256]) + dot(left2[q], delta[q, 256:512])
    tail = jnp.concatenate([*heads, jnp.zeros((14, 512), f32)], axis=0).astype(bf16)
    for d in range(8):
        wide = slice(64 * d, 64 * d + 64)
        thin = slice(512 + 16 * d, 528 + 16 * d)
        out[d, 0:64, :] = grad[0, wide, :].astype(bf16)
        out[d, 64:128, :] = grad[1, wide, :].astype(bf16)
        out[d, 128:144, :] = grad[0, thin, :].astype(bf16)
        out[d, 144:160, :] = grad[1, thin, :].astype(bf16)
        out[d, 160:176, :] = tail
    push = dot(slope0[...], p[...])
    first, second = push[0:128], push[128:256]
    keep[0] = jnp.where(core == 1, second, first)
    give[0] = jnp.where(core == 1, first, second)
    first, second = push[256:384], push[384:512]
    keep[1] = jnp.where(core == 1, second, first)
    give[1] = jnp.where(core == 1, first, second)


def total_body(got, w, chunk0, chunk1, act, head):
    def at(rows):
        x = [got[d, rows, :].astype(f32) for d in range(8)]
        return ((x[0] + x[1]) + (x[2] + x[3])) + ((x[4] + x[5]) + (x[6] + x[7]))

    total = at(slice(0, 64)).astype(bf16)
    for d in range(8):
        chunk0[d] = total
    chunk1[...] = at(slice(64, 128)).astype(bf16)
    head[...] = at(slice(160, 168))
    for q in range(2):
        m = at(slice(128 + 16 * q, 144 + 16 * q)).astype(bf16)
        act[16 * q : 16 * q + 16, :] = lax.dot_general(
            m, w[q], (((1,), (1,)), ((), ())), preferred_element_type=f32
        )


def second_body(chunk1, act1, act2, out):
    act = (act1[...] + act2[...]).astype(bf16)
    for d in range(8):
        out[d, 0:64, :] = chunk1[...]
        out[d, 64:96, :] = act


def renew(q, g, cin, tin, fresh, blended, c, t, isems, osems):
    ins, outs = [], []
    for h in range(2):
        rows = slice(256 * h, 256 * h + 256)
        ins.append(pltpu.make_async_copy(cin.at[q, rows], c.at[rows], isems.at[0, h]))
        ins.append(pltpu.make_async_copy(tin.at[q, rows], t.at[rows], isems.at[1, h]))
        outs.append(pltpu.make_async_copy(c.at[rows], fresh.at[q, rows], osems.at[0, h]))
        outs.append(pltpu.make_async_copy(t.at[rows], blended.at[q, rows], osems.at[1, h]))

    def work(h):
        for d in range(4 * h, 4 * h + 4):
            at = slice(64 * d, 64 * d + 64)
            new = c[at, :] - matrix_rate * g[d, 0:64, :].astype(f32)
            c[at, :] = new
            t[at, :] = blend_rate * new + (1.0 - blend_rate) * t[at, :]

    return ins, outs, work


def update0_body(g, cin, tin, fresh, blended, c, t, isems, osems):
    ins, outs, work = renew(0, g, cin, tin, fresh, blended, c, t, isems, osems)
    for copy in ins:
        copy.start()
    for h in range(2):
        ins[2 * h].wait()
        ins[2 * h + 1].wait()
        work(h)
        outs[2 * h].start()
        outs[2 * h + 1].start()
    for copy in outs:
        copy.wait()


def update1_body(
    g, cin, tin, cact, tact, fresh0, blended0, fresh, blended, fresh_act, blended_act,
    c, t, ca, ta, isems, osems, asems,
):
    ins, outs, work = renew(1, g, cin, tin, fresh, blended, c, t, isems, osems)
    more = [
        pltpu.make_async_copy(cact, ca, asems.at[0]),
        pltpu.make_async_copy(tact, ta, asems.at[1]),
    ]
    last = [
        pltpu.make_async_copy(ca, fresh_act, asems.at[2]),
        pltpu.make_async_copy(ta, blended_act, asems.at[3]),
    ]
    for copy in ins + more:
        copy.start()
    for h in range(2):
        ins[2 * h].wait()
        ins[2 * h + 1].wait()
        work(h)
        outs[2 * h].start()
        outs[2 * h + 1].start()
    for copy in more:
        copy.wait()
    for d in range(8):
        for q in range(2):
            rows = slice(16 * d, 16 * d + 16)
            term = g[d, 64 + 16 * q : 80 + 16 * q, :].astype(f32)
            new = ca[q, rows, :] - matrix_rate * term
            ca[q, rows, :] = new
            ta[q, rows, :] = blend_rate * new + (1.0 - blend_rate) * ta[q, rows, :]
    for copy in last:
        copy.start()
    for copy in outs + last:
        copy.wait()


def on_device(
    observed,
    next_observed,
    actions,
    next_mean,
    policy_noise,
    rewards,
    discounts,
    actor_flags,
    critic_in,
    critic_act,
    critic_head,
    target_in,
    target_act,
    target_head,
):
    row, col, dp = lax.axis_index("row"), lax.axis_index("col"), lax.axis_index("dp")
    at = jnp.stack([row % 2, col, row // 2, dp]).astype(jnp.int32)

    (own,) = call(
        pack_body,
        [shape(128, 1280)],
        [observed, next_observed, actions, next_mean, policy_noise],
        scratch=[pltpu.VMEM((128, 128), bf16), pltpu.VMEM((128, 128), f32), DMA((5,))],
        mib=4, raw=range(5), name="pack",
    )
    sib = swap(own, "row", 1)
    far = swap(own, "row", 2)
    w16, a16, p16 = call(
        weights_body,
        [shape(4, 512, 512), shape(4, 128, 512), shape(512, 128)],
        [critic_in, target_in, critic_act, target_act],
        scratch=[pltpu.VMEM((4, 512, 512), f32), pltpu.VMEM((4, 128, 512), f32), DMA((8,))],
        mib=16, flops=2 * 128 * 512 * 512, raw=range(4), to=(2,), name="weights",
    )

    def forward(x0, x1, name):
        return call(
            forward_body,
            [
                shape(64, 2048, dtype=f32), shape(64, 2048), shape(64, 2048), shape(64, 2048),
                shape(2, 640, 256),
            ],
            [x0, x1, a16, w16],
            scratch=[pltpu.VMEM((256, 1280), bf16), pltpu.VMEM((256, 2048), f32)],
            scalars=at, flops=8 * 256 * 640 * 512, to=range(5), name=name,
        )

    mine1, *out1, left1 = forward(own, sib, "forward_near")
    in1 = [None, None, None]
    for k in (2, 1, 3):
        in1[k - 1] = swap(out1[k - 1], "col", k)
    far = after(far, mine1)
    farsib = swap(far, "row", 1)
    mine2, *out2, left2 = forward(far, farsib, "forward_far")
    in2 = [None, None, None]
    for k in (2, 1, 3):
        in2[k - 1] = swap(out2[k - 1], "col", k)
    heads = jnp.concatenate([critic_head, target_head, jnp.zeros((4, 512), f32)], axis=0)
    blank = jnp.zeros((1, 128), f32)
    rew = jnp.concatenate(
        [blank, blank, blank, blank, rewards.astype(f32)[None], discounts.astype(f32)[None], blank, blank]
    )
    slope, hidden, packet = call(
        hidden_body,
        [shape(128, 1024), shape(128, 1024, dtype=f32), shape(16, 8, 128, dtype=f32)],
        [mine1, *in1, mine2, *in2, heads, rew],
        scratch=[pltpu.VMEM((128, 128), f32)],
        scalars=at, where=(0, 4), to=range(3), name="hidden", flops=128 * 2048 * 30,
    )
    slopes = [slope] + [swap(slope, "col", k) for k in (1, 2, 3)]
    got = lax.all_to_all(packet, ("row", "col"), 0, 0, tiled=True)
    grads, keep, give, temporal_errors = call(
        grads_body,
        [
            shape(8, 176, 512), shape(2, 128, 128, dtype=f32),
            shape(2, 128, 128, dtype=f32), shape(2, 128, dtype=f32),
        ],
        [*slopes, got, left1, left2, hidden, p16],
        scratch=[
            pltpu.VMEM((2, 512, 512), bf16), pltpu.VMEM((512, 512), bf16),
            pltpu.VMEM((2, 640, 512), f32), pltpu.VMEM((4, 8, 128), f32),
        ],
        scalars=at, where=(0, 5, 6, 7, 8), to=range(4), name="grads", flops=4 * 640 * 512 * 512,
    )
    parts = lax.all_to_all(grads, "dp", 0, 0, tiled=True)
    push = keep + swap(give, "row", 1)
    push = push[0] + swap(push[1], "row", 2)

    chunk0, chunk1, act, head = call(
        total_body,
        [shape(8, 64, 512), shape(64, 512), shape(32, 512, dtype=f32), shape(8, 512, dtype=f32)],
        [parts, w16], to=range(4), name="total", flops=4 * 16 * 512 * 512,
    )
    grad0 = lax.all_to_all(chunk0, "dp", 0, 0, tiled=True)
    act = act + swap(act, "row", 1)
    (chunk1,) = call(
        second_body, [shape(8, 96, 512)], [chunk1, act, swap(act, "row", 2)],
        where=(0,), to=(0,), name="second",
    )
    grad1 = lax.all_to_all(chunk1, "dp", 0, 0, tiled=True)
    both = jnp.concatenate([push, head[0:2].reshape(8, 128)], axis=0)
    both = both + swap(both, "col", 1)
    both = both + swap(both, "col", 2)
    action_slope = actor_flags.astype(f32)[:, None] * both[0:128]
    head = both[128:136].reshape(2, 512)
    wide, thin = shape(2, 512, 512, dtype=f32), shape(2, 128, 512, dtype=f32)
    big, small = pltpu.VMEM((512, 512), f32), pltpu.VMEM((2, 128, 512), f32)
    new_in, new_target_in = call(
        update0_body, [wide, wide], [grad0, critic_in, target_in],
        scratch=[big, big, DMA((2, 2)), DMA((2, 2))],
        raw=(1, 2), to="raw", mib=8, name="update_first",
    )
    new_in, new_target_in, new_act, new_target_act = call(
        update1_body, [wide, wide, thin, thin],
        [grad1, critic_in, target_in, critic_act, target_act, new_in, new_target_in],
        scratch=[big, big, small, small, DMA((2, 2)), DMA((2, 2)), DMA((4,))],
        raw=range(1, 7), to="raw", mib=8, aliases={5: 0, 6: 1}, name="update_second",
    )
    new_head = critic_head - head_rate * head
    new_target_head = blend_rate * new_head + (1.0 - blend_rate) * target_head
    return (
        new_in,
        new_act,
        new_head,
        new_target_in,
        new_target_act,
        new_target_head,
        temporal_errors,
        action_slope,
    )


def solution(mesh):
    return jax.shard_map(
        on_device,
        mesh=mesh,
        in_specs=(
            P(("row", "dp"), "col"),
            P(("row", "dp"), "col"),
            P(("row", "dp"), None),
            P(("row", "dp"), None),
            P(("row", "dp"), None),
            P(("row", "dp")),
            P(("row", "dp")),
            P(("row", "dp")),
            P(None, "col", "row"),
            P(None, None, "col"),
            P(None, "row"),
            P(None, "col", "row"),
            P(None, None, "col"),
            P(None, "row"),
        ),
        out_specs=(
            P(None, "col", "row"),
            P(None, None, "col"),
            P(None, "row"),
            P(None, "col", "row"),
            P(None, None, "col"),
            P(None, "row"),
            P(None, ("row", "dp")),
            P(("row", "dp"), None),
        ),
        check_vma=False,
    )
```

```python
import jax
import jax.numpy as jnp
from jax import lax
from jax.experimental import pallas as pl
from jax.experimental.pallas import tpu as pltpu
from jax.sharding import PartitionSpec as P

noise_clip = 0.5
matrix_rate = 0.004
head_rate = 0.0001
blend_rate = 0.005

bf16 = jnp.bfloat16
f32 = jnp.float32

SPECS = {m: pl.BlockSpec(memory_space=m) for m in (pltpu.VMEM, pltpu.SMEM, pltpu.HBM)}
DMA = pltpu.SemaphoreType.DMA
VMEM, HBM = pltpu.VMEM, pltpu.HBM


def call(
    body, outs, ins, scratch=(), scalars=None, mib=16, flops=0, name=None,
    where=(), to=(), raw=(), raw_out=(),
):
    moved = sum(a.size * a.dtype.itemsize for a in ins)
    moved += sum(o.size * o.dtype.itemsize for o in outs)
    specs = [SPECS[HBM if i in raw else VMEM] for i in range(len(ins))]
    ins = [
        pltpu.with_memory_space_constraint(a, HBM) if i in raw or i in where else a
        for i, a in enumerate(ins)
    ]
    if scalars is not None:
        ins = [scalars, *ins]
        specs = [SPECS[pltpu.SMEM], *specs]
    return pl.pallas_call(
        body,
        out_shape=tuple(HBM(o.shape, o.dtype) if i in to else o for i, o in enumerate(outs)),
        in_specs=specs,
        out_specs=tuple(SPECS[HBM if i in raw_out else VMEM] for i in range(len(outs))),
        scratch_shapes=list(scratch),
        compiler_params=pltpu.CompilerParams(vmem_limit_bytes=mib * 2**20),
        cost_estimate=pl.CostEstimate(flops=flops, bytes_accessed=moved, transcendentals=0),
        name=name,
    )(*ins)


def after(x, other):
    return pl.pallas_call(
        lambda x, other, out: None,
        out_shape=HBM(x.shape, x.dtype),
        in_specs=[SPECS[HBM], SPECS[HBM]],
        out_specs=SPECS[HBM],
        input_output_aliases={0: 0},
        name="after",
    )(pltpu.with_memory_space_constraint(x, HBM), pltpu.with_memory_space_constraint(other, HBM))


def shape(*dims, dtype=bf16):
    return jax.ShapeDtypeStruct(dims, dtype)


def dot(a, b):
    return jnp.dot(a, b, preferred_element_type=f32)


def swap(x, axis, bit):
    n = lax.axis_size(axis)
    return lax.ppermute(x, axis, [(i, i ^ bit) for i in range(n)])


def pack_body(obs, nxt, act, mean, noise, out, means, noises, sems):
    copies = [
        pltpu.make_async_copy(src, dst, sems.at[i])
        for i, (src, dst) in enumerate(
            (
                (mean, means),
                (noise, noises),
                (obs, out.at[:, 0:512]),
                (nxt, out.at[:, 512:1024]),
                (act, out.at[:, 1024:1152]),
            )
        )
    ]
    for c in copies:
        c.start()
    copies[0].wait()
    copies[1].wait()
    clipped = jnp.clip(noises[...], -noise_clip, noise_clip)
    out[:, 1152:1280] = jnp.clip(means[...].astype(f32) + clipped, -1.0, 1.0).astype(bf16)
    for c in copies[2:]:
        c.wait()


def weights_body(cin, tin, cact, tact, w, a, p, wide, thin, sems):
    pairs = []
    for k in range(2):
        pairs.append((cact.at[k], thin.at[k]))
        pairs.append((cin.at[k], wide.at[k]))
    for k in range(2):
        pairs.append((tact.at[k], thin.at[2 + k]))
        pairs.append((tin.at[k], wide.at[2 + k]))
    copies = [pltpu.make_async_copy(src, dst, sems.at[i]) for i, (src, dst) in enumerate(pairs)]
    for c in copies:
        c.start()
    for k in range(4):
        copies[2 * k].wait()
        a[k] = thin[k].astype(bf16)
        copies[2 * k + 1].wait()
        w[k] = wide[k].astype(bf16)
        if k == 0:
            p[...] = dot(a[0], w[0]).T.astype(bf16)


def forward_body(at, x0, x1, a, w, mine, out1, out2, out3, left, turned, xs, part):
    core, col = at[0], at[1]
    xs[pl.ds(pl.multiple_of(core * 128, 128), 128), :] = x0[...]
    xs[pl.ds(pl.multiple_of((1 - core) * 128, 128), 128), :] = x1[...]
    turned[...] = xs[:, 1024:1152].T
    for q in range(4):
        s = 0 if q < 2 else 512
        m = 1024 if q < 2 else 1152
        e = (xs[:, s : s + 512].astype(f32) + dot(xs[:, m : m + 128], a[q])).astype(bf16)
        if q < 2:
            left[q] = e.T
        part[:, 512 * q : 512 * q + 512] = dot(e, w[q])

    def rows(k):
        return pl.ds(pl.multiple_of((col ^ k) * 64, 64), 64)

    mine[...] = part[rows(0), :]
    out1[...] = part[rows(1), :].astype(bf16)
    out2[...] = part[rows(2), :].astype(bf16)
    out3[...] = part[rows(3), :].astype(bf16)


def hidden_body(at, m1, r11, r12, r13, m2, r21, r22, r23, heads, rew, slope, hidden, packet, vals):
    y_hi = at[2]
    vals[...] = jnp.zeros_like(vals)
    for half, (m, r1, r2, r3) in enumerate(((m1, r11, r12, r13), (m2, r21, r22, r23))):
        rows = slice(64 * half, 64 * half + 64)
        for q in range(4):
            cols = slice(512 * q, 512 * q + 512)
            pre = (m[:, cols] + r1[:, cols].astype(f32)) + (
                r2[:, cols].astype(f32) + r3[:, cols].astype(f32)
            )
            sig = jax.nn.sigmoid(pre)
            hid = pre * sig
            v = heads[q : q + 1, :]
            vals[rows, q : q + 1] = jnp.sum(hid * v, axis=1, keepdims=True)
            if q < 2:
                hidden[rows, cols] = hid
                slope[rows, cols] = (v * (sig * (1.0 + pre * (1.0 - sig)))).astype(bf16)
    turned = vals[...].T[0:8, :]
    swapped = jnp.concatenate([turned[:, 64:128], turned[:, 0:64]], axis=1)
    turned = jnp.where(y_hi == 1, swapped, turned)
    line = lax.broadcasted_iota(jnp.int32, (8, 128), 0)
    turned = jnp.where(line < 4, turned, rew[...])
    for i in range(16):
        packet[i] = turned


def errors_body(
    at, s0, s1, s2, s3, got, turned1, turned2, hidden, p,
    out, delta, keep, give, terr,
    slope0, errs,
):
    core, col, y_hi = at[0], at[1], at[2]
    for c in range(4):
        v = (got[c] + got[4 + c]) + (got[8 + c] + got[12 + c])
        lanes = slice(64 * (c % 2), 64 * (c % 2) + 64)
        both = jnp.concatenate([got[c // 2 * 4][:, lanes], got[(2 + c // 2) * 4][:, lanes]], axis=1)
        goal = both[4:5] + both[5:6] * jnp.minimum(v[2:3], v[3:4])
        e = v[0:2] - goal
        e = jnp.where(y_hi == 1, jnp.concatenate([e[:, 64:128], e[:, 0:64]], axis=1), e)
        errs[c, 0:2, :] = e
    lo = jnp.concatenate([errs[0, 0:2, 0:64], errs[1, 0:2, 0:64]], axis=1)
    hi = jnp.concatenate([errs[2, 0:2, 0:64], errs[3, 0:2, 0:64]], axis=1)
    terr[...] = jnp.where(core == 1, hi, lo)
    for k, s in enumerate((s0, s1, s2, s3)):
        c = col ^ k
        block = jnp.concatenate([errs[c], jnp.zeros((120, 128), f32)], axis=0)
        e = 2.0 * block.T
        for half in range(2):
            rows = slice(64 * half, 64 * half + 64)
            to = pl.ds(pl.multiple_of(256 * half + 64 * c, 64), 64)
            slope0[to, :] = s[rows, 0:512]
            for q in range(2):
                cols = slice(512 * q, 512 * q + 512)
                delta[q, to, :] = (e[rows, q : q + 1] * s[rows, cols].astype(f32)).astype(bf16)
        if k == 0:
            heads = [
                jnp.sum(e[:, q : q + 1] * hidden[:, 512 * q : 512 * q + 512], axis=0, keepdims=True)
                for q in range(2)
            ]
    tail = jnp.concatenate([*heads, jnp.zeros((14, 512), f32)], axis=0).astype(bf16)
    for q in range(2):
        m = dot(turned1[...], delta[q, 0:256]) + dot(turned2[...], delta[q, 256:512])
        for d in range(8):
            out[d, 16 * q : 16 * q + 16, :] = m[16 * d : 16 * d + 16, :].astype(bf16)
    for d in range(8):
        out[d, 32:48, :] = tail
    push = dot(slope0[...], p[...])
    for chip in range(2):
        first, second = push[256 * chip : 256 * chip + 128], push[256 * chip + 128 : 256 * chip + 256]
        rows = slice(128 * chip, 128 * chip + 128)
        keep[rows, :] = jnp.where(core == 1, second, first)
        give[rows, :] = jnp.where(core == 1, first, second)


def grads_body(left1, left2, delta, out):
    for q in range(2):
        grad = dot(left1[q], delta[q, 0:256]) + dot(left2[q], delta[q, 256:512])
        for d in range(8):
            out[d, 64 * q : 64 * q + 64, :] = grad[64 * d : 64 * d + 64, :].astype(bf16)


def summed(got, rows):
    x = [got[d, rows, :].astype(f32) for d in range(8)]
    return ((x[0] + x[1]) + (x[2] + x[3])) + ((x[4] + x[5]) + (x[6] + x[7]))


def action_body(got, w, keep, give, mine, theirs):
    for q in range(2):
        m = summed(got, slice(16 * q, 16 * q + 16)).astype(bf16)
        term = lax.dot_general(m, w[q], (((1,), (1,)), ((), ())), preferred_element_type=f32)
        for j in range(4):
            i = 16 * (4 * q + j)
            mine[i : i + 16, :] = term[:, 128 * j : 128 * j + 128]
            theirs[i : i + 16, :] = term[:, 128 * j : 128 * j + 128]
    mine[128:384, :] = keep[...]
    theirs[128:384, :] = give[...]
    heads = summed(got, slice(32, 40))
    for q in range(2):
        for j in range(4):
            i = 384 + 4 * q + j
            mine[i : i + 1, :] = heads[q : q + 1, 128 * j : 128 * j + 128]
    theirs[384:392, :] = jnp.zeros((8, 128), f32)


def fold_body(mine, other, high, low, own):
    total = mine[0:128, :] + other[0:128, :]
    high[0:128, :] = total
    low[...] = total
    high[128:256, :] = mine[256:384, :] + other[256:384, :]
    own[0:128, :] = mine[128:256, :] + other[128:256, :]
    own[128:136, :] = mine[384:392, :]


def pair_body(high, low, own, from_high, from_low, from_both, pair, rest):
    sums = (low[...] + from_high[0:128, :], from_low[...] + from_both[...])
    for m, total in enumerate(sums):
        for q in range(2):
            for j in range(4):
                i = 16 * (4 * q + j)
                lanes = slice(128 * j, 128 * j + 128)
                pair[m, 16 * q : 16 * q + 16, lanes] = total[i : i + 16, :].astype(bf16)
    rest[0:128, :] = own[0:128, :] + from_high[128:256, :]
    rest[128:136, :] = own[128:136, :]


def total_body(got, pair, chunk):
    total = summed(got, slice(0, 128)).astype(bf16)
    for d in range(8):
        chunk[d] = total


def update_body(
    at, g, g0, g1, g2, g3, cin, tin, cact, tact,
    fresh, blended, fresh_act, blended_act,
    c, t, ca, ta, isems, osems, asems,
):
    dp = at[3]
    places = [(q, slice(256 * h, 256 * h + 256)) for q in range(2) for h in range(2)]
    ins, outs = [], []
    for i, (q, rows) in enumerate(places):
        ins.append(pltpu.make_async_copy(cin.at[q, rows], c.at[q, rows], isems.at[0, i]))
        ins.append(pltpu.make_async_copy(tin.at[q, rows], t.at[q, rows], isems.at[1, i]))
        outs.append(pltpu.make_async_copy(c.at[q, rows], fresh.at[q, rows], osems.at[0, i]))
        outs.append(pltpu.make_async_copy(t.at[q, rows], blended.at[q, rows], osems.at[1, i]))
    more = [
        pltpu.make_async_copy(cact, ca, asems.at[0]),
        pltpu.make_async_copy(tact, ta, asems.at[1]),
    ]
    last = [
        pltpu.make_async_copy(ca, fresh_act, asems.at[2]),
        pltpu.make_async_copy(ta, blended_act, asems.at[3]),
    ]
    for copy in ins + more:
        copy.start()
    for i, (q, rows) in enumerate(places):
        ins[2 * i].wait()
        ins[2 * i + 1].wait()
        for d in range(rows.start // 64, rows.stop // 64):
            part = slice(64 * d, 64 * d + 64)
            new = c[q, part, :] - matrix_rate * g[d, 64 * q : 64 * q + 64, :].astype(f32)
            c[q, part, :] = new
            t[q, part, :] = blend_rate * new + (1.0 - blend_rate) * t[q, part, :]
        outs[2 * i].start()
        outs[2 * i + 1].start()
    for copy in more:
        copy.wait()
    for k, piece in enumerate((g0, g1, g2, g3)):
        for m in range(2):
            rows = pl.ds(pl.multiple_of((dp ^ (4 * m + k)) * 16, 16), 16)
            for q in range(2):
                new = ca[q, rows, :] - matrix_rate * piece[m, 16 * q : 16 * q + 16, :].astype(f32)
                ca[q, rows, :] = new
                ta[q, rows, :] = blend_rate * new + (1.0 - blend_rate) * ta[q, rows, :]
    for copy in last:
        copy.start()
    for copy in last + outs:
        copy.wait()


def on_device(
    observed,
    next_observed,
    actions,
    next_mean,
    policy_noise,
    rewards,
    discounts,
    actor_flags,
    critic_in,
    critic_act,
    critic_head,
    target_in,
    target_act,
    target_head,
):
    row, col, dp = lax.axis_index("row"), lax.axis_index("col"), lax.axis_index("dp")
    at = jnp.stack([row % 2, col, row // 2, dp]).astype(jnp.int32)

    (own,) = call(
        pack_body,
        [shape(128, 1280)],
        [observed, next_observed, actions, next_mean, policy_noise],
        scratch=[pltpu.VMEM((128, 128), bf16), pltpu.VMEM((128, 128), f32), DMA((5,))],
        mib=4, raw=range(5), name="pack",
    )
    sib = swap(own, "row", 1)
    far = swap(own, "row", 2)
    w16, a16, p16 = call(
        weights_body,
        [shape(4, 512, 512), shape(4, 128, 512), shape(512, 128)],
        [critic_in, target_in, critic_act, target_act],
        scratch=[pltpu.VMEM((4, 512, 512), f32), pltpu.VMEM((4, 128, 512), f32), DMA((8,))],
        mib=16, flops=2 * 128 * 512 * 512, raw=range(4), to=(2,), name="weights",
    )

    def forward(x0, x1, name, where, to):
        return call(
            forward_body,
            [
                shape(64, 2048, dtype=f32), shape(64, 2048), shape(64, 2048), shape(64, 2048),
                shape(2, 512, 256), shape(128, 256),
            ],
            [x0, x1, a16, w16],
            scratch=[pltpu.VMEM((256, 1280), bf16), pltpu.VMEM((256, 2048), f32)],
            scalars=at, flops=8 * 256 * 640 * 512, where=where, to=to, name=name,
        )

    mine1, *out1, left1, turned1 = forward(own, sib, "forward_near", (), range(6))
    in1 = [None, None, None]
    for k in (2, 1, 3):
        in1[k - 1] = swap(out1[k - 1], "col", k)
    far = after(far, mine1)
    farsib = swap(far, "row", 1)
    mine2, *out2, left2, turned2 = forward(far, farsib, "forward_far", (0,), (0, 4, 5))
    in2 = [None, None, None]
    for k in (2, 1, 3):
        in2[k - 1] = swap(out2[k - 1], "col", k)
    heads = jnp.concatenate([critic_head, target_head, jnp.zeros((4, 512), f32)], axis=0)
    blank = jnp.zeros((1, 128), f32)
    rew = jnp.concatenate(
        [blank, blank, blank, blank, rewards.astype(f32)[None], discounts.astype(f32)[None], blank, blank]
    )
    slope, hidden, packet = call(
        hidden_body,
        [shape(128, 1024), shape(128, 1024, dtype=f32), shape(16, 8, 128, dtype=f32)],
        [mine1, *in1, mine2, *in2, heads, rew],
        scratch=[pltpu.VMEM((128, 128), f32)],
        scalars=at, where=(0, 4), to=(1,), name="hidden", flops=128 * 2048 * 30,
    )
    slopes = [slope] + [swap(slope, "col", k) for k in (1, 2, 3)]
    got = lax.all_to_all(packet, ("row", "col"), 0, 0, tiled=True)
    moves, delta, keep, give, temporal_errors = call(
        errors_body,
        [
            shape(8, 48, 512), shape(2, 512, 512), shape(256, 128, dtype=f32),
            shape(256, 128, dtype=f32), shape(2, 128, dtype=f32),
        ],
        [*slopes, got, turned1, turned2, hidden, p16],
        scratch=[pltpu.VMEM((512, 512), bf16), pltpu.VMEM((4, 8, 128), f32)],
        scalars=at, where=(5, 6, 7, 8), to=(0, 2, 3), name="errors",
        flops=6 * 128 * 512 * 512,
    )
    moves = lax.all_to_all(moves, "dp", 0, 0, tiled=True)
    (grads,) = call(
        grads_body, [shape(8, 128, 512)], [left1, left2, delta],
        where=(0, 1), name="grads", flops=4 * 512 * 512 * 512,
    )
    parts = lax.all_to_all(grads, "dp", 0, 0, tiled=True)
    mine, theirs = call(
        action_body, [shape(392, 128, dtype=f32)] * 2, [moves, w16, keep, give],
        where=(2, 3), name="action", flops=4 * 16 * 512 * 512,
    )
    high, low, own = call(
        fold_body,
        [shape(256, 128, dtype=f32), shape(128, 128, dtype=f32), shape(136, 128, dtype=f32)],
        [mine, swap(theirs, "row", 1)], name="fold",
    )
    from_high = swap(high, "row", 2)
    from_low = swap(low, "dp", 4)
    from_both = lax.ppermute(low, ("row", "dp"), [(i, i ^ 20) for i in range(32)])
    pair, rest = call(
        pair_body, [shape(2, 32, 512), shape(136, 128, dtype=f32)],
        [high, low, own, from_high, from_low, from_both], name="pair",
    )
    (chunk,) = call(total_body, [shape(8, 128, 512)], [parts, pair], name="total")
    grad_in = lax.all_to_all(chunk, "dp", 0, 0, tiled=True)
    pairs = [pair] + [swap(pair, "dp", k) for k in (1, 2, 3)]
    rest = rest + swap(rest, "col", 1)
    rest = rest + swap(rest, "col", 2)
    action_slope = actor_flags.astype(f32)[:, None] * rest[0:128]
    head = rest[128:136].reshape(2, 512)
    new_head = critic_head - head_rate * head
    new_target_head = blend_rate * new_head + (1.0 - blend_rate) * target_head
    wide, thin = shape(2, 512, 512, dtype=f32), shape(2, 128, 512, dtype=f32)
    big, small = pltpu.VMEM((2, 512, 512), f32), pltpu.VMEM((2, 128, 512), f32)
    new_in, new_target_in, new_act, new_target_act = call(
        update_body, [wide, wide, thin, thin],
        [grad_in, *pairs, critic_in, target_in, critic_act, target_act],
        scratch=[big, big, small, small, DMA((2, 4)), DMA((2, 4)), DMA((4,))],
        scalars=at, raw=range(5, 9), raw_out=range(4), to=range(4), name="update",
    )
    return (
        new_in,
        new_act,
        new_head,
        new_target_in,
        new_target_act,
        new_target_head,
        temporal_errors,
        action_slope,
    )


def solution(mesh):
    return jax.shard_map(
        on_device,
        mesh=mesh,
        in_specs=(
            P(("row", "dp"), "col"),
            P(("row", "dp"), "col"),
            P(("row", "dp"), None),
            P(("row", "dp"), None),
            P(("row", "dp"), None),
            P(("row", "dp")),
            P(("row", "dp")),
            P(("row", "dp")),
            P(None, "col", "row"),
            P(None, None, "col"),
            P(None, "row"),
            P(None, "col", "row"),
            P(None, None, "col"),
            P(None, "row"),
        ),
        out_specs=(
            P(None, "col", "row"),
            P(None, None, "col"),
            P(None, "row"),
            P(None, "col", "row"),
            P(None, None, "col"),
            P(None, "row"),
            P(None, ("row", "dp")),
            P(("row", "dp"), None),
        ),
        check_vma=False,
    )
```

```python
import jax
import jax.numpy as jnp
from jax import lax
from jax.experimental import pallas as pl
from jax.experimental.pallas import tpu as pltpu
from jax.sharding import PartitionSpec as P

noise_clip = 0.5
matrix_rate = 0.004
head_rate = 0.0001
blend_rate = 0.005

bf16 = jnp.bfloat16
f32 = jnp.float32

SPECS = {m: pl.BlockSpec(memory_space=m) for m in (pltpu.VMEM, pltpu.SMEM, pltpu.HBM)}
DMA = pltpu.SemaphoreType.DMA
VMEM, HBM = pltpu.VMEM, pltpu.HBM


def call(
    body, outs, ins, scratch=(), scalars=None, mib=16, flops=0, name=None,
    where=(), to=(), raw=(), raw_out=(), aliases=None,
):
    moved = sum(a.size * a.dtype.itemsize for a in ins)
    moved += sum(o.size * o.dtype.itemsize for o in outs)
    specs = [SPECS[HBM if i in raw else VMEM] for i in range(len(ins))]
    ins = [
        pltpu.with_memory_space_constraint(a, HBM) if i in raw or i in where else a
        for i, a in enumerate(ins)
    ]
    if scalars is not None:
        ins = [scalars, *ins]
        specs = [SPECS[pltpu.SMEM], *specs]
    return pl.pallas_call(
        body,
        out_shape=tuple(HBM(o.shape, o.dtype) if i in to else o for i, o in enumerate(outs)),
        in_specs=specs,
        out_specs=tuple(SPECS[HBM if i in raw_out else VMEM] for i in range(len(outs))),
        scratch_shapes=list(scratch),
        input_output_aliases=aliases or {},
        compiler_params=pltpu.CompilerParams(vmem_limit_bytes=mib * 2**20),
        cost_estimate=pl.CostEstimate(flops=flops, bytes_accessed=moved, transcendentals=0),
        name=name,
    )(*ins)


def after(x, other):
    return pl.pallas_call(
        lambda x, other, out: None,
        out_shape=HBM(x.shape, x.dtype),
        in_specs=[SPECS[HBM], SPECS[HBM]],
        out_specs=SPECS[HBM],
        input_output_aliases={0: 0},
        name="after",
    )(pltpu.with_memory_space_constraint(x, HBM), pltpu.with_memory_space_constraint(other, HBM))


def shape(*dims, dtype=bf16):
    return jax.ShapeDtypeStruct(dims, dtype)


def dot(a, b):
    return jnp.dot(a, b, preferred_element_type=f32)


def swap(x, axis, bit):
    n = lax.axis_size(axis)
    return lax.ppermute(x, axis, [(i, i ^ bit) for i in range(n)])


def pack_body(obs, nxt, act, mean, noise, out, means, noises, sems):
    copies = [
        pltpu.make_async_copy(src, dst, sems.at[i])
        for i, (src, dst) in enumerate(
            (
                (mean, means),
                (noise, noises),
                (obs, out.at[:, 0:512]),
                (nxt, out.at[:, 512:1024]),
                (act, out.at[:, 1024:1152]),
            )
        )
    ]
    for c in copies:
        c.start()
    copies[0].wait()
    copies[1].wait()
    clipped = jnp.clip(noises[...], -noise_clip, noise_clip)
    out[:, 1152:1280] = jnp.clip(means[...].astype(f32) + clipped, -1.0, 1.0).astype(bf16)
    for c in copies[2:]:
        c.wait()


def weights_body(cin, tin, cact, tact, w, a, p, wide, thin, sems):
    pairs = []
    for k in range(2):
        pairs.append((cact.at[k], thin.at[k]))
        pairs.append((cin.at[k], wide.at[k]))
    for k in range(2):
        pairs.append((tact.at[k], thin.at[2 + k]))
        pairs.append((tin.at[k], wide.at[2 + k]))
    copies = [pltpu.make_async_copy(src, dst, sems.at[i]) for i, (src, dst) in enumerate(pairs)]
    for c in copies:
        c.start()
    for k in range(4):
        copies[2 * k].wait()
        a[k] = thin[k].astype(bf16)
        copies[2 * k + 1].wait()
        w[k] = wide[k].astype(bf16)
        if k == 0:
            p[...] = dot(a[0], w[0]).T.astype(bf16)


def forward_body(at, x0, x1, a, w, mine, out1, out2, out3, left, xs, part):
    core, col = at[0], at[1]
    xs[pl.ds(pl.multiple_of(core * 128, 128), 128), :] = x0[...]
    xs[pl.ds(pl.multiple_of((1 - core) * 128, 128), 128), :] = x1[...]
    turned = xs[:, 1024:1152].T
    for q in range(4):
        s = 0 if q < 2 else 512
        m = 1024 if q < 2 else 1152
        e = (xs[:, s : s + 512].astype(f32) + dot(xs[:, m : m + 128], a[q])).astype(bf16)
        if q < 2:
            left[q, 0:512, :] = e.T
            left[q, 512:640, :] = turned
        part[:, 512 * q : 512 * q + 512] = dot(e, w[q])

    def rows(k):
        return pl.ds(pl.multiple_of((col ^ k) * 64, 64), 64)

    mine[...] = part[rows(0), :]
    out1[...] = part[rows(1), :].astype(bf16)
    out2[...] = part[rows(2), :].astype(bf16)
    out3[...] = part[rows(3), :].astype(bf16)


def hidden_body(at, m1, r11, r12, r13, m2, r21, r22, r23, heads, rew, slope, hidden, packet, vals):
    y_hi = at[2]
    vals[...] = jnp.zeros_like(vals)
    for half, (m, r1, r2, r3) in enumerate(((m1, r11, r12, r13), (m2, r21, r22, r23))):
        rows = slice(64 * half, 64 * half + 64)
        for q in range(4):
            cols = slice(512 * q, 512 * q + 512)
            pre = (m[:, cols] + r1[:, cols].astype(f32)) + (
                r2[:, cols].astype(f32) + r3[:, cols].astype(f32)
            )
            sig = jax.nn.sigmoid(pre)
            hid = pre * sig
            v = heads[q : q + 1, :]
            vals[rows, q : q + 1] = jnp.sum(hid * v, axis=1, keepdims=True)
            if q < 2:
                hidden[rows, cols] = hid
                slope[rows, cols] = (v * (sig * (1.0 + pre * (1.0 - sig)))).astype(bf16)
    turned = vals[...].T[0:8, :]
    swapped = jnp.concatenate([turned[:, 64:128], turned[:, 0:64]], axis=1)
    turned = jnp.where(y_hi == 1, swapped, turned)
    line = lax.broadcasted_iota(jnp.int32, (8, 128), 0)
    turned = jnp.where(line < 4, turned, rew[...])
    for i in range(16):
        packet[i] = turned


def grads_body(
    at, s0, s1, s2, s3, got, left1, left2, hidden, p,
    out, keep, give, terr,
    delta, slope0, grad, errs,
):
    core, col, y_hi = at[0], at[1], at[2]
    for c in range(4):
        v = (got[c] + got[4 + c]) + (got[8 + c] + got[12 + c])
        lanes = slice(64 * (c % 2), 64 * (c % 2) + 64)
        both = jnp.concatenate([got[c // 2 * 4][:, lanes], got[(2 + c // 2) * 4][:, lanes]], axis=1)
        goal = both[4:5] + both[5:6] * jnp.minimum(v[2:3], v[3:4])
        e = v[0:2] - goal
        e = jnp.where(y_hi == 1, jnp.concatenate([e[:, 64:128], e[:, 0:64]], axis=1), e)
        errs[c, 0:2, :] = e
    lo = jnp.concatenate([errs[0, 0:2, 0:64], errs[1, 0:2, 0:64]], axis=1)
    hi = jnp.concatenate([errs[2, 0:2, 0:64], errs[3, 0:2, 0:64]], axis=1)
    terr[...] = jnp.where(core == 1, hi, lo)
    for k, s in enumerate((s0, s1, s2, s3)):
        c = col ^ k
        block = jnp.concatenate([errs[c], jnp.zeros((120, 128), f32)], axis=0)
        e = 2.0 * block.T
        for half in range(2):
            rows = slice(64 * half, 64 * half + 64)
            to = pl.ds(pl.multiple_of(256 * half + 64 * c, 64), 64)
            slope0[to, :] = s[rows, 0:512]
            for q in range(2):
                cols = slice(512 * q, 512 * q + 512)
                delta[q, to, :] = (e[rows, q : q + 1] * s[rows, cols].astype(f32)).astype(bf16)
        if k == 0:
            heads = [
                jnp.sum(e[:, q : q + 1] * hidden[:, 512 * q : 512 * q + 512], axis=0, keepdims=True)
                for q in range(2)
            ]
    for q in range(2):
        grad[q] = dot(left1[q], delta[q, 0:256]) + dot(left2[q], delta[q, 256:512])
    for d in range(8):
        wide = slice(64 * d, 64 * d + 64)
        thin = slice(512 + 16 * d, 528 + 16 * d)
        out[d, 0:64, :] = grad[0, wide, :].astype(bf16)
        out[d, 64:128, :] = grad[1, wide, :].astype(bf16)
        out[d, 128:144, :] = grad[0, thin, :].astype(bf16)
        out[d, 144:160, :] = grad[1, thin, :].astype(bf16)
    push = dot(slope0[...], p[...])
    for chip in range(2):
        first, second = push[256 * chip : 256 * chip + 128], push[256 * chip + 128 : 256 * chip + 256]
        rows = slice(128 * chip, 128 * chip + 128)
        keep[rows, :] = jnp.where(core == 1, second, first)
        give[rows, :] = jnp.where(core == 1, first, second)
    for q in range(2):
        for j in range(4):
            i = 256 + 4 * q + j
            keep[i : i + 1, :] = heads[q][:, 128 * j : 128 * j + 128]
    give[256:264, :] = jnp.zeros((8, 128), f32)


def summed(got, rows):
    x = [got[d, rows, :].astype(f32) for d in range(8)]
    return ((x[0] + x[1]) + (x[2] + x[3])) + ((x[4] + x[5]) + (x[6] + x[7]))


def action_body(got, w, t, act):
    for q in range(2):
        m = summed(got, slice(128 + 16 * q, 144 + 16 * q)).astype(bf16)
        term = lax.dot_general(m, w[q], (((1,), (1,)), ((), ())), preferred_element_type=f32)
        for j in range(4):
            i = 16 * (4 * q + j)
            act[i : i + 16, :] = term[:, 128 * j : 128 * j + 128]


def fold_body(act, other, t, high):
    high[0:128, :] = act[...] + other[...]
    high[128:256, :] = t[128:256, :]


def first_body(got, act, chunk):
    total = summed(got, slice(0, 64)).astype(bf16)
    for d in range(8):
        chunk[d] = total


def second_body(got, high, from_high, t, chunk):
    total = summed(got, slice(64, 128)).astype(bf16)
    act = (high[0:128, :] + from_high[0:128, :]).astype(bf16)
    lines = []
    for q in range(2):
        line = jnp.concatenate([t[256 + 4 * q + j : 257 + 4 * q + j, :] for j in range(4)], axis=1)
        lines.append(jnp.broadcast_to(line, (8, 512)))
    heads = jnp.concatenate(lines, axis=0).astype(bf16)
    for d in range(8):
        chunk[d, 0:64, :] = total
        for q in range(2):
            for j in range(4):
                i = 16 * (4 * q + j)
                chunk[d, 64 + 16 * q : 80 + 16 * q, 128 * j : 128 * j + 128] = act[i : i + 16, :]
        chunk[d, 96:112, :] = heads


def renew(q, g, cin, tin, fresh, blended, c, t, isems, osems, between=None):
    ins, outs = [], []
    for h in range(2):
        rows = slice(256 * h, 256 * h + 256)
        ins.append(pltpu.make_async_copy(cin.at[q, rows], c.at[rows], isems.at[0, h]))
        ins.append(pltpu.make_async_copy(tin.at[q, rows], t.at[rows], isems.at[1, h]))
        outs.append(pltpu.make_async_copy(c.at[rows], fresh.at[q, rows], osems.at[0, h]))
        outs.append(pltpu.make_async_copy(t.at[rows], blended.at[q, rows], osems.at[1, h]))
    for copy in ins:
        copy.start()
    for h in range(2):
        ins[2 * h].wait()
        ins[2 * h + 1].wait()
        for d in range(4 * h, 4 * h + 4):
            part = slice(64 * d, 64 * d + 64)
            new = c[part, :] - matrix_rate * g[d, 0:64, :].astype(f32)
            c[part, :] = new
            t[part, :] = blend_rate * new + (1.0 - blend_rate) * t[part, :]
        outs[2 * h].start()
        outs[2 * h + 1].start()
    if between is not None:
        between()
    for copy in outs:
        copy.wait()


def update_first_body(g, cin, tin, fresh, blended, c, t, isems, osems):
    renew(0, g, cin, tin, fresh, blended, c, t, isems, osems)


def update_second_body(
    g, chead, thead, cin, tin, cact, tact, fresh0, blended0,
    fresh, blended, fresh_act, blended_act, fresh_head, blended_head,
    c, t, ca, ta, isems, osems, asems,
):
    more = [
        pltpu.make_async_copy(cact, ca, asems.at[0]),
        pltpu.make_async_copy(tact, ta, asems.at[1]),
    ]
    last = [
        pltpu.make_async_copy(ca, fresh_act, asems.at[2]),
        pltpu.make_async_copy(ta, blended_act, asems.at[3]),
    ]
    for copy in more:
        copy.start()
    for q in range(2):
        total = summed(g, slice(96 + 8 * q, 104 + 8 * q))
        new = chead[q : q + 1, :] - head_rate * total[0:1, :]
        fresh_head[q : q + 1, :] = new
        blended_head[q : q + 1, :] = blend_rate * new + (1.0 - blend_rate) * thead[q : q + 1, :]

    def action_part():
        for copy in more:
            copy.wait()
        for d in range(8):
            rows = slice(16 * d, 16 * d + 16)
            for q in range(2):
                part = g[d, 64 + 16 * q : 80 + 16 * q, :].astype(f32)
                new = ca[q, rows, :] - matrix_rate * part
                ca[q, rows, :] = new
                ta[q, rows, :] = blend_rate * new + (1.0 - blend_rate) * ta[q, rows, :]
        for copy in last:
            copy.start()

    renew(1, g, cin, tin, fresh, blended, c, t, isems, osems, action_part)
    for copy in last:
        copy.wait()


def on_device(
    observed,
    next_observed,
    actions,
    next_mean,
    policy_noise,
    rewards,
    discounts,
    actor_flags,
    critic_in,
    critic_act,
    critic_head,
    target_in,
    target_act,
    target_head,
):
    row, col, dp = lax.axis_index("row"), lax.axis_index("col"), lax.axis_index("dp")
    at = jnp.stack([row % 2, col, row // 2, dp]).astype(jnp.int32)

    (own,) = call(
        pack_body,
        [shape(128, 1280)],
        [observed, next_observed, actions, next_mean, policy_noise],
        scratch=[pltpu.VMEM((128, 128), bf16), pltpu.VMEM((128, 128), f32), DMA((5,))],
        mib=4, raw=range(5), name="pack",
    )
    sib = swap(own, "row", 1)
    far = swap(own, "row", 2)
    w16, a16, p16 = call(
        weights_body,
        [shape(4, 512, 512), shape(4, 128, 512), shape(512, 128)],
        [critic_in, target_in, critic_act, target_act],
        scratch=[pltpu.VMEM((4, 512, 512), f32), pltpu.VMEM((4, 128, 512), f32), DMA((8,))],
        mib=16, flops=2 * 128 * 512 * 512, raw=range(4), to=(2,), name="weights",
    )

    def forward(x0, x1, name, where, to):
        return call(
            forward_body,
            [
                shape(64, 2048, dtype=f32), shape(64, 2048), shape(64, 2048), shape(64, 2048),
                shape(2, 640, 256),
            ],
            [x0, x1, a16, w16],
            scratch=[pltpu.VMEM((256, 1280), bf16), pltpu.VMEM((256, 2048), f32)],
            scalars=at, flops=8 * 256 * 640 * 512, where=where, to=to, name=name,
        )

    mine1, *out1, left1 = forward(own, sib, "forward_near", (), range(5))
    in1 = [None, None, None]
    for k in (2, 1, 3):
        in1[k - 1] = swap(out1[k - 1], "col", k)
    far = after(far, mine1)
    farsib = swap(far, "row", 1)
    mine2, *out2, left2 = forward(far, farsib, "forward_far", (0,), (0, 4))
    in2 = [None, None, None]
    for k in (2, 1, 3):
        in2[k - 1] = swap(out2[k - 1], "col", k)
    heads = jnp.concatenate([critic_head, target_head, jnp.zeros((4, 512), f32)], axis=0)
    blank = jnp.zeros((1, 128), f32)
    rew = jnp.concatenate(
        [blank, blank, blank, blank, rewards.astype(f32)[None], discounts.astype(f32)[None], blank, blank]
    )
    slope, hidden, packet = call(
        hidden_body,
        [shape(128, 1024), shape(128, 1024, dtype=f32), shape(16, 8, 128, dtype=f32)],
        [mine1, *in1, mine2, *in2, heads, rew],
        scratch=[pltpu.VMEM((128, 128), f32)],
        scalars=at, where=(0, 4), to=(1,), name="hidden", flops=128 * 2048 * 30,
    )
    slopes = [slope] + [swap(slope, "col", k) for k in (1, 2, 3)]
    got = lax.all_to_all(packet, ("row", "col"), 0, 0, tiled=True)
    grads, keep, give, temporal_errors = call(
        grads_body,
        [
            shape(8, 160, 512), shape(264, 128, dtype=f32),
            shape(264, 128, dtype=f32), shape(2, 128, dtype=f32),
        ],
        [*slopes, got, left1, left2, hidden, p16],
        scratch=[
            pltpu.VMEM((2, 512, 512), bf16), pltpu.VMEM((512, 512), bf16),
            pltpu.VMEM((2, 640, 512), f32), pltpu.VMEM((4, 8, 128), f32),
        ],
        scalars=at, where=(5, 6, 7, 8), to=range(4), name="grads", flops=4 * 640 * 512 * 512,
    )
    parts = lax.all_to_all(grads, "dp", 0, 0, tiled=True)
    t = keep + swap(give, "row", 1)
    t = t + swap(t, "col", 1)
    t = t + swap(t, "col", 2)

    (act,) = call(
        action_body, [shape(128, 128, dtype=f32)], [parts, w16, t],
        to=(0,), name="action", flops=4 * 16 * 512 * 512,
    )
    (chunk0,) = call(first_body, [shape(8, 64, 512)], [parts, act], where=(1,), to=(0,), name="first")
    grad0 = lax.all_to_all(chunk0, "dp", 0, 0, tiled=True)
    (high,) = call(
        fold_body, [shape(256, 128, dtype=f32)], [act, swap(act, "row", 1), t], where=(0,), name="fold"
    )
    from_high = swap(high, "row", 2)
    (chunk1,) = call(
        second_body, [shape(8, 112, 512)], [parts, high, from_high, t], to=(0,), name="second"
    )
    grad1 = lax.all_to_all(chunk1, "dp", 0, 0, tiled=True)
    action_slope = actor_flags.astype(f32)[:, None] * (t[0:128] + from_high[128:256])
    wide, thin, line = shape(2, 512, 512, dtype=f32), shape(2, 128, 512, dtype=f32), shape(2, 512, dtype=f32)
    big, small = pltpu.VMEM((512, 512), f32), pltpu.VMEM((2, 128, 512), f32)
    new_in, new_target_in = call(
        update_first_body, [wide, wide], [grad0, critic_in, target_in],
        scratch=[big, big, DMA((2, 2)), DMA((2, 2))],
        raw=(1, 2), raw_out=range(2), to=range(2), mib=8, name="update_first",
    )
    new_in, new_target_in, new_act, new_target_act, new_head, new_target_head = call(
        update_second_body, [wide, wide, thin, thin, line, line],
        [
            grad1, critic_head, target_head,
            critic_in, target_in, critic_act, target_act, new_in, new_target_in,
        ],
        scratch=[big, big, small, small, DMA((2, 2)), DMA((2, 2)), DMA((4,))],
        where=(1, 2), raw=range(3, 9), raw_out=range(4), to=range(6), mib=8,
        aliases={7: 0, 8: 1}, name="update_second",
    )
    return (
        new_in,
        new_act,
        new_head,
        new_target_in,
        new_target_act,
        new_target_head,
        temporal_errors,
        action_slope,
    )


def solution(mesh):
    return jax.shard_map(
        on_device,
        mesh=mesh,
        in_specs=(
            P(("row", "dp"), "col"),
            P(("row", "dp"), "col"),
            P(("row", "dp"), None),
            P(("row", "dp"), None),
            P(("row", "dp"), None),
            P(("row", "dp")),
            P(("row", "dp")),
            P(("row", "dp")),
            P(None, "col", "row"),
            P(None, None, "col"),
            P(None, "row"),
            P(None, "col", "row"),
            P(None, None, "col"),
            P(None, "row"),
        ),
        out_specs=(
            P(None, "col", "row"),
            P(None, None, "col"),
            P(None, "row"),
            P(None, "col", "row"),
            P(None, None, "col"),
            P(None, "row"),
            P(None, ("row", "dp")),
            P(("row", "dp"), None),
        ),
        check_vma=False,
    )
```

```python
import jax
import jax.numpy as jnp
from jax import lax
from jax.experimental import pallas as pl
from jax.experimental.pallas import tpu as pltpu
from jax.sharding import PartitionSpec as P

noise_clip = 0.5
matrix_rate = 0.004
head_rate = 0.0001
blend_rate = 0.005

bf16 = jnp.bfloat16
f32 = jnp.float32

SPECS = {m: pl.BlockSpec(memory_space=m) for m in (pltpu.VMEM, pltpu.SMEM, pltpu.HBM)}
DMA = pltpu.SemaphoreType.DMA
VMEM, HBM = pltpu.VMEM, pltpu.HBM


def call(
    body, outs, ins, scratch=(), scalars=None, mib=16, flops=0, name=None,
    where=(), to=(), raw=(), raw_out=(),
):
    moved = sum(a.size * a.dtype.itemsize for a in ins)
    moved += sum(o.size * o.dtype.itemsize for o in outs)
    specs = [SPECS[HBM if i in raw else VMEM] for i in range(len(ins))]
    ins = [
        pltpu.with_memory_space_constraint(a, HBM) if i in raw or i in where else a
        for i, a in enumerate(ins)
    ]
    if scalars is not None:
        ins = [scalars, *ins]
        specs = [SPECS[pltpu.SMEM], *specs]
    return pl.pallas_call(
        body,
        out_shape=tuple(HBM(o.shape, o.dtype) if i in to else o for i, o in enumerate(outs)),
        in_specs=specs,
        out_specs=tuple(SPECS[HBM if i in raw_out else VMEM] for i in range(len(outs))),
        scratch_shapes=list(scratch),
        compiler_params=pltpu.CompilerParams(vmem_limit_bytes=mib * 2**20),
        cost_estimate=pl.CostEstimate(flops=flops, bytes_accessed=moved, transcendentals=0),
        name=name,
    )(*ins)


def after(x, other):
    return pl.pallas_call(
        lambda x, other, out: None,
        out_shape=HBM(x.shape, x.dtype),
        in_specs=[SPECS[HBM], SPECS[HBM]],
        out_specs=SPECS[HBM],
        input_output_aliases={0: 0},
        name="after",
    )(pltpu.with_memory_space_constraint(x, HBM), pltpu.with_memory_space_constraint(other, HBM))


def shape(*dims, dtype=bf16):
    return jax.ShapeDtypeStruct(dims, dtype)


def dot(a, b):
    return jnp.dot(a, b, preferred_element_type=f32)


def swap(x, axis, bit):
    n = lax.axis_size(axis)
    return lax.ppermute(x, axis, [(i, i ^ bit) for i in range(n)])


def pack_body(obs, nxt, act, mean, noise, out, means, noises, sems):
    copies = [
        pltpu.make_async_copy(src, dst, sems.at[i])
        for i, (src, dst) in enumerate(
            (
                (mean, means),
                (noise, noises),
                (obs, out.at[:, 0:512]),
                (nxt, out.at[:, 512:1024]),
                (act, out.at[:, 1024:1152]),
            )
        )
    ]
    for c in copies:
        c.start()
    copies[0].wait()
    copies[1].wait()
    clipped = jnp.clip(noises[...], -noise_clip, noise_clip)
    out[:, 1152:1280] = jnp.clip(means[...].astype(f32) + clipped, -1.0, 1.0).astype(bf16)
    for c in copies[2:]:
        c.wait()


def weights_body(cin, tin, cact, tact, w, a, p, wide, thin, sems):
    pairs = []
    for k in range(2):
        pairs.append((cact.at[k], thin.at[k]))
        pairs.append((cin.at[k], wide.at[k]))
    for k in range(2):
        pairs.append((tact.at[k], thin.at[2 + k]))
        pairs.append((tin.at[k], wide.at[2 + k]))
    copies = [pltpu.make_async_copy(src, dst, sems.at[i]) for i, (src, dst) in enumerate(pairs)]
    for c in copies:
        c.start()
    for k in range(4):
        copies[2 * k].wait()
        a[k] = thin[k].astype(bf16)
        copies[2 * k + 1].wait()
        w[k] = wide[k].astype(bf16)
        if k == 0:
            p[...] = dot(a[0], w[0]).T.astype(bf16)


def forward_body(at, x0, x1, a, w, mine, out1, out2, out3, left, turned, xs, part):
    core, col = at[0], at[1]
    xs[pl.ds(pl.multiple_of(core * 128, 128), 128), :] = x0[...]
    xs[pl.ds(pl.multiple_of((1 - core) * 128, 128), 128), :] = x1[...]
    turned[...] = xs[:, 1024:1152].T
    for q in range(4):
        s = 0 if q < 2 else 512
        m = 1024 if q < 2 else 1152
        e = (xs[:, s : s + 512].astype(f32) + dot(xs[:, m : m + 128], a[q])).astype(bf16)
        if q < 2:
            left[q] = e.T
        part[:, 512 * q : 512 * q + 512] = dot(e, w[q])

    def rows(k):
        return pl.ds(pl.multiple_of((col ^ k) * 64, 64), 64)

    mine[...] = part[rows(0), :]
    out1[...] = part[rows(1), :].astype(bf16)
    out2[...] = part[rows(2), :].astype(bf16)
    out3[...] = part[rows(3), :].astype(bf16)


def hidden_body(at, m1, r11, r12, r13, m2, r21, r22, r23, heads, rew, slope, hidden, packet, vals):
    y_hi = at[2]
    vals[...] = jnp.zeros_like(vals)
    for half, (m, r1, r2, r3) in enumerate(((m1, r11, r12, r13), (m2, r21, r22, r23))):
        rows = slice(64 * half, 64 * half + 64)
        for q in range(4):
            cols = slice(512 * q, 512 * q + 512)
            pre = (m[:, cols] + r1[:, cols].astype(f32)) + (
                r2[:, cols].astype(f32) + r3[:, cols].astype(f32)
            )
            sig = jax.nn.sigmoid(pre)
            hid = pre * sig
            v = heads[q : q + 1, :]
            vals[rows, q : q + 1] = jnp.sum(hid * v, axis=1, keepdims=True)
            if q < 2:
                hidden[rows, cols] = hid
                slope[rows, cols] = (v * (sig * (1.0 + pre * (1.0 - sig)))).astype(bf16)
    turned = vals[...].T[0:8, :]
    swapped = jnp.concatenate([turned[:, 64:128], turned[:, 0:64]], axis=1)
    turned = jnp.where(y_hi == 1, swapped, turned)
    line = lax.broadcasted_iota(jnp.int32, (8, 128), 0)
    turned = jnp.where(line < 4, turned, rew[...])
    for i in range(16):
        packet[i] = turned


def errors_body(
    at, s0, s1, s2, s3, got, turned1, turned2, hidden, p,
    out, delta, keep, give, terr,
    slope0, errs,
):
    core, col, y_hi = at[0], at[1], at[2]
    for c in range(4):
        v = (got[c] + got[4 + c]) + (got[8 + c] + got[12 + c])
        lanes = slice(64 * (c % 2), 64 * (c % 2) + 64)
        both = jnp.concatenate([got[c // 2 * 4][:, lanes], got[(2 + c // 2) * 4][:, lanes]], axis=1)
        goal = both[4:5] + both[5:6] * jnp.minimum(v[2:3], v[3:4])
        e = v[0:2] - goal
        e = jnp.where(y_hi == 1, jnp.concatenate([e[:, 64:128], e[:, 0:64]], axis=1), e)
        errs[c, 0:2, :] = e
    lo = jnp.concatenate([errs[0, 0:2, 0:64], errs[1, 0:2, 0:64]], axis=1)
    hi = jnp.concatenate([errs[2, 0:2, 0:64], errs[3, 0:2, 0:64]], axis=1)
    terr[...] = jnp.where(core == 1, hi, lo)
    for k, s in enumerate((s0, s1, s2, s3)):
        c = col ^ k
        block = jnp.concatenate([errs[c], jnp.zeros((120, 128), f32)], axis=0)
        e = 2.0 * block.T
        for half in range(2):
            rows = slice(64 * half, 64 * half + 64)
            to = pl.ds(pl.multiple_of(256 * half + 64 * c, 64), 64)
            slope0[to, :] = s[rows, 0:512]
            for q in range(2):
                cols = slice(512 * q, 512 * q + 512)
                delta[q, to, :] = (e[rows, q : q + 1] * s[rows, cols].astype(f32)).astype(bf16)
        if k == 0:
            heads = [
                jnp.sum(e[:, q : q + 1] * hidden[:, 512 * q : 512 * q + 512], axis=0, keepdims=True)
                for q in range(2)
            ]
    tail = jnp.concatenate([*heads, jnp.zeros((14, 512), f32)], axis=0).astype(bf16)
    for q in range(2):
        m = dot(turned1[...], delta[q, 0:256]) + dot(turned2[...], delta[q, 256:512])
        for d in range(8):
            out[d, 16 * q : 16 * q + 16, :] = m[16 * d : 16 * d + 16, :].astype(bf16)
    for d in range(8):
        out[d, 32:48, :] = tail
    push = dot(slope0[...], p[...])
    for chip in range(2):
        first, second = push[256 * chip : 256 * chip + 128], push[256 * chip + 128 : 256 * chip + 256]
        rows = slice(128 * chip, 128 * chip + 128)
        keep[rows, :] = jnp.where(core == 1, second, first)
        give[rows, :] = jnp.where(core == 1, first, second)


def grads_body(left1, left2, delta, out):
    for q in range(2):
        grad = dot(left1[q], delta[q, 0:256]) + dot(left2[q], delta[q, 256:512])
        for d in range(8):
            out[d, 64 * q : 64 * q + 64, :] = grad[64 * d : 64 * d + 64, :].astype(bf16)


def summed(got, rows):
    x = [got[d, rows, :].astype(f32) for d in range(8)]
    return ((x[0] + x[1]) + (x[2] + x[3])) + ((x[4] + x[5]) + (x[6] + x[7]))


def action_body(got, w, keep, give, mine, theirs):
    for q in range(2):
        m = summed(got, slice(16 * q, 16 * q + 16)).astype(bf16)
        term = lax.dot_general(m, w[q], (((1,), (1,)), ((), ())), preferred_element_type=f32)
        for j in range(4):
            i = 16 * (4 * q + j)
            mine[i : i + 16, :] = term[:, 128 * j : 128 * j + 128]
            theirs[i : i + 16, :] = term[:, 128 * j : 128 * j + 128]
    mine[128:384, :] = keep[...]
    theirs[128:384, :] = give[...]
    heads = summed(got, slice(32, 40))
    for q in range(2):
        for j in range(4):
            i = 384 + 4 * q + j
            mine[i : i + 1, :] = heads[q : q + 1, 128 * j : 128 * j + 128]
    theirs[384:392, :] = jnp.zeros((8, 128), f32)


def fold_body(mine, other, high, low, own):
    total = mine[0:128, :] + other[0:128, :]
    high[0:128, :] = total
    low[...] = total
    high[128:256, :] = mine[256:384, :] + other[256:384, :]
    own[0:128, :] = mine[128:256, :] + other[128:256, :]
    own[128:136, :] = mine[384:392, :]


def pair_body(high, low, own, from_high, from_low, from_both, pair, rest):
    sums = (low[...] + from_high[0:128, :], from_low[...] + from_both[...])
    for m, total in enumerate(sums):
        for q in range(2):
            for j in range(4):
                i = 16 * (4 * q + j)
                lanes = slice(128 * j, 128 * j + 128)
                pair[m, 16 * q : 16 * q + 16, lanes] = total[i : i + 16, :].astype(bf16)
    rest[0:128, :] = own[0:128, :] + from_high[128:256, :]
    rest[128:136, :] = own[128:136, :]


def total_body(got, pair, chunk):
    total = summed(got, slice(0, 128)).astype(bf16)
    for d in range(8):
        chunk[d] = total


def update_body(
    at, g, g0, g1, g2, g3, cin, tin, cact, tact,
    fresh, blended, fresh_act, blended_act,
    c, t, ca, ta, isems, osems, asems,
):
    dp = at[3]
    places = [(q, slice(256 * h, 256 * h + 256)) for q in range(2) for h in range(2)]
    ins, outs = [], []
    for i, (q, rows) in enumerate(places):
        ins.append(pltpu.make_async_copy(cin.at[q, rows], c.at[q, rows], isems.at[0, i]))
        ins.append(pltpu.make_async_copy(tin.at[q, rows], t.at[q, rows], isems.at[1, i]))
        outs.append(pltpu.make_async_copy(c.at[q, rows], fresh.at[q, rows], osems.at[0, i]))
        outs.append(pltpu.make_async_copy(t.at[q, rows], blended.at[q, rows], osems.at[1, i]))
    more = [
        pltpu.make_async_copy(cact, ca, asems.at[0]),
        pltpu.make_async_copy(tact, ta, asems.at[1]),
    ]
    last = [
        pltpu.make_async_copy(ca, fresh_act, asems.at[2]),
        pltpu.make_async_copy(ta, blended_act, asems.at[3]),
    ]
    for copy in ins + more:
        copy.start()
    for i, (q, rows) in enumerate(places):
        ins[2 * i].wait()
        ins[2 * i + 1].wait()
        for d in range(rows.start // 64, rows.stop // 64):
            part = slice(64 * d, 64 * d + 64)
            new = c[q, part, :] - matrix_rate * g[d, 64 * q : 64 * q + 64, :].astype(f32)
            c[q, part, :] = new
            t[q, part, :] = blend_rate * new + (1.0 - blend_rate) * t[q, part, :]
        outs[2 * i].start()
        outs[2 * i + 1].start()
    for copy in more:
        copy.wait()
    for k, piece in enumerate((g0, g1, g2, g3)):
        for m in range(2):
            rows = pl.ds(pl.multiple_of((dp ^ (4 * m + k)) * 16, 16), 16)
            for q in range(2):
                new = ca[q, rows, :] - matrix_rate * piece[m, 16 * q : 16 * q + 16, :].astype(f32)
                ca[q, rows, :] = new
                ta[q, rows, :] = blend_rate * new + (1.0 - blend_rate) * ta[q, rows, :]
    for copy in last:
        copy.start()
    for copy in last + outs:
        copy.wait()


def on_device(
    observed,
    next_observed,
    actions,
    next_mean,
    policy_noise,
    rewards,
    discounts,
    actor_flags,
    critic_in,
    critic_act,
    critic_head,
    target_in,
    target_act,
    target_head,
):
    row, col, dp = lax.axis_index("row"), lax.axis_index("col"), lax.axis_index("dp")
    at = jnp.stack([row % 2, col, row // 2, dp]).astype(jnp.int32)

    (own,) = call(
        pack_body,
        [shape(128, 1280)],
        [observed, next_observed, actions, next_mean, policy_noise],
        scratch=[pltpu.VMEM((128, 128), bf16), pltpu.VMEM((128, 128), f32), DMA((5,))],
        mib=4, raw=range(5), name="pack",
    )
    sib = swap(own, "row", 1)
    far = swap(own, "row", 2)
    w16, a16, p16 = call(
        weights_body,
        [shape(4, 512, 512), shape(4, 128, 512), shape(512, 128)],
        [critic_in, target_in, critic_act, target_act],
        scratch=[pltpu.VMEM((4, 512, 512), f32), pltpu.VMEM((4, 128, 512), f32), DMA((8,))],
        mib=16, flops=2 * 128 * 512 * 512, raw=range(4), to=(2,), name="weights",
    )

    def forward(x0, x1, name, where, to):
        return call(
            forward_body,
            [
                shape(64, 2048, dtype=f32), shape(64, 2048), shape(64, 2048), shape(64, 2048),
                shape(2, 512, 256), shape(128, 256),
            ],
            [x0, x1, a16, w16],
            scratch=[pltpu.VMEM((256, 1280), bf16), pltpu.VMEM((256, 2048), f32)],
            scalars=at, flops=8 * 256 * 640 * 512, where=where, to=to, name=name,
        )

    mine1, *out1, left1, turned1 = forward(own, sib, "forward_near", (), range(6))
    in1 = [None, None, None]
    for k in (2, 1, 3):
        in1[k - 1] = swap(out1[k - 1], "col", k)
    far = after(far, mine1)
    farsib = swap(far, "row", 1)
    mine2, *out2, left2, turned2 = forward(far, farsib, "forward_far", (0,), (0, 4, 5))
    in2 = [None, None, None]
    for k in (2, 1, 3):
        in2[k - 1] = swap(out2[k - 1], "col", k)
    heads = jnp.concatenate([critic_head, target_head, jnp.zeros((4, 512), f32)], axis=0)
    blank = jnp.zeros((1, 128), f32)
    rew = jnp.concatenate(
        [blank, blank, blank, blank, rewards.astype(f32)[None], discounts.astype(f32)[None], blank, blank]
    )
    slope, hidden, packet = call(
        hidden_body,
        [shape(128, 1024), shape(128, 1024, dtype=f32), shape(16, 8, 128, dtype=f32)],
        [mine1, *in1, mine2, *in2, heads, rew],
        scratch=[pltpu.VMEM((128, 128), f32)],
        scalars=at, where=(0, 4), to=(1,), name="hidden", flops=128 * 2048 * 30,
    )
    slopes = [slope] + [swap(slope, "col", k) for k in (1, 2, 3)]
    got = lax.all_to_all(packet, ("row", "col"), 0, 0, tiled=True)
    moves, delta, keep, give, temporal_errors = call(
        errors_body,
        [
            shape(8, 48, 512), shape(2, 512, 512), shape(256, 128, dtype=f32),
            shape(256, 128, dtype=f32), shape(2, 128, dtype=f32),
        ],
        [*slopes, got, turned1, turned2, hidden, p16],
        scratch=[pltpu.VMEM((512, 512), bf16), pltpu.VMEM((4, 8, 128), f32)],
        scalars=at, where=(5, 6, 7, 8), to=(0, 2, 3), name="errors",
        flops=6 * 128 * 512 * 512,
    )
    moves = lax.all_to_all(moves, "dp", 0, 0, tiled=True)
    (grads,) = call(
        grads_body, [shape(8, 128, 512)], [left1, left2, delta],
        where=(0, 1), name="grads", flops=4 * 512 * 512 * 512,
    )
    parts = lax.all_to_all(grads, "dp", 0, 0, tiled=True)
    mine, theirs = call(
        action_body, [shape(392, 128, dtype=f32)] * 2, [moves, w16, keep, give],
        where=(2, 3), name="action", flops=4 * 16 * 512 * 512,
    )
    high, low, own = call(
        fold_body,
        [shape(256, 128, dtype=f32), shape(128, 128, dtype=f32), shape(136, 128, dtype=f32)],
        [mine, swap(theirs, "row", 1)], name="fold",
    )
    from_high = swap(high, "row", 2)
    from_low = swap(low, "dp", 4)
    from_both = lax.ppermute(low, ("row", "dp"), [(i, i ^ 20) for i in range(32)])
    pair, rest = call(
        pair_body, [shape(2, 32, 512), shape(136, 128, dtype=f32)],
        [high, low, own, from_high, from_low, from_both], name="pair",
    )
    (chunk,) = call(total_body, [shape(8, 128, 512)], [parts, pair], name="total")
    grad_in = lax.all_to_all(chunk, "dp", 0, 0, tiled=True)
    pairs = [pair] + [swap(pair, "dp", k) for k in (1, 2, 3)]
    terms = [swap(rest, "col", k) for k in (1, 2, 3)]
    rest = (rest + terms[0]) + (terms[1] + terms[2])
    action_slope = actor_flags.astype(f32)[:, None] * rest[0:128]
    head = rest[128:136].reshape(2, 512)
    new_head = critic_head - head_rate * head
    new_target_head = blend_rate * new_head + (1.0 - blend_rate) * target_head
    wide, thin = shape(2, 512, 512, dtype=f32), shape(2, 128, 512, dtype=f32)
    big, small = pltpu.VMEM((2, 512, 512), f32), pltpu.VMEM((2, 128, 512), f32)
    new_in, new_target_in, new_act, new_target_act = call(
        update_body, [wide, wide, thin, thin],
        [grad_in, *pairs, critic_in, target_in, critic_act, target_act],
        scratch=[big, big, small, small, DMA((2, 4)), DMA((2, 4)), DMA((4,))],
        scalars=at, raw=range(5, 9), raw_out=range(4), to=range(4), name="update",
    )
    return (
        new_in,
        new_act,
        new_head,
        new_target_in,
        new_target_act,
        new_target_head,
        temporal_errors,
        action_slope,
    )


def solution(mesh):
    return jax.shard_map(
        on_device,
        mesh=mesh,
        in_specs=(
            P(("row", "dp"), "col"),
            P(("row", "dp"), "col"),
            P(("row", "dp"), None),
            P(("row", "dp"), None),
            P(("row", "dp"), None),
            P(("row", "dp")),
            P(("row", "dp")),
            P(("row", "dp")),
            P(None, "col", "row"),
            P(None, None, "col"),
            P(None, "row"),
            P(None, "col", "row"),
            P(None, None, "col"),
            P(None, "row"),
        ),
        out_specs=(
            P(None, "col", "row"),
            P(None, None, "col"),
            P(None, "row"),
            P(None, "col", "row"),
            P(None, None, "col"),
            P(None, "row"),
            P(None, ("row", "dp")),
            P(("row", "dp"), None),
        ),
        check_vma=False,
    )
```
